32 devices in a mesh: grp: 4 (over y, x), shard: 8 (over z, core).
Axes of the slice: x: 2, y: 2, z: 4, core: 2. Of those that a mesh axis runs over, the one named last changes fastest.
Arguments:
- cells: bfloat16 [128, 64, 768], P('shard'), may hold values from -8 to 8
- w_cell: bfloat16 [768, 768], replicated, may hold values from -0.21875 to 0.21875
- w_mix: bfloat16 [768, 768], replicated, may hold values from -0.21875 to 0.21875
- w_pool: bfloat16 [768, 768], replicated, may hold values from -0.21875 to 0.21875
- pairs: int32 [2048, 2], P(('grp', 'shard')), may hold values from 0 to 127, as said below
- counts: int32 [32], P(('grp', 'shard')), may hold values from 1 to 64, 1536 in all
Outputs:
- scores: float32 [2048], P(('grp', 'shard'))
The draws below stay inside these ranges and needn't reach their ends.
Inputs may be any that keep to these rules, and one draw needn't show every extreme that they name: Column c lies on shard index c // 16. The first column of each pair of reader r lies on shard index r % 8. Among the 64 pairs of one reader at most 16 have their second column on one shard index, and on some shard index exactly 16. The two columns of a pair differ.
All inputs are finite; a program needn't handle non-finite values. No bound on the sum of `counts` on one device may be relied on, other than what follows from the above.
Results may differ from the reference program's by a relative error of at most 0.0014.
Values may be sent and summed in bfloat16 or wider, within the bound.
No kernel may reach another device: no remote copies, remote signals or barrier semaphores. Data moves between devices by JAX's collectives and lax.ppermute only.
A program may use at most 192 MiB of HBM per device.

```python
import math
import jax
import jax.numpy as jnp
import numpy as np
from jax import lax

WIDTH = 768
SAMPLES = 64
COLUMNS_PER_SHARD = 16
PAIR_DEV = 64
COLS = 128
READERS = 32
PAIRS = 2048
CAP = 16


def draw_cells(key, part):
    base_key = jax.random.fold_in(key, 0)
    value_rows = jnp.clip(jax.random.normal(base_key, (COLS, SAMPLES, WIDTH), jnp.float32), -6.0, 6.0)
    return value_rows.astype(jnp.bfloat16)


def draw_pairs(key, part):
    shards = COLS // COLUMNS_PER_SHARD
    readers = PAIRS // PAIR_DEV

    def one_reader(reader):
        reader_key = jax.random.fold_in(key, reader)
        keys = jax.random.split(reader_key, 6)
        home = reader % shards
        left_local = jax.random.randint(keys[0], (PAIR_DEV,), 0, COLUMNS_PER_SHARD)
        first_owner = jax.random.randint(keys[1], (), 0, shards)
        spread = jax.random.permutation(keys[2], CAP * (shards - 1))[:PAIR_DEV - CAP]
        others = (spread % (shards - 1) + first_owner + 1) % shards
        owners = jnp.concatenate([jnp.full((CAP,), first_owner, jnp.int32), others.astype(jnp.int32)])
        owners = jax.random.permutation(keys[3], owners)
        drawn = jax.random.randint(keys[4], (PAIR_DEV,), 0, COLUMNS_PER_SHARD)
        shifted = (left_local + 1 + jax.random.randint(keys[5], (PAIR_DEV,), 0, COLUMNS_PER_SHARD - 1)) % COLUMNS_PER_SHARD
        right_local = jnp.where(owners == home, shifted, drawn)
        left_ids = home * COLUMNS_PER_SHARD + left_local
        right_ids = owners * COLUMNS_PER_SHARD + right_local
        return jnp.stack([left_ids, right_ids], axis=1)
    return jax.vmap(one_reader)(jnp.arange(readers)).reshape(PAIRS, 2).astype(jnp.int32)


def split_up(number_of, total, limit, skew):
    weights = [(1 << 20) // math.isqrt(rank ** skew) + 1 for rank in range(2, number_of + 1)]
    spare, holding = total - limit - (number_of - 1), [1] * (number_of - 1)
    while spare > 0:
        movable = [i for i in range(number_of - 1) if holding[i] < limit]
        mass, remaining = sum([weights[i] for i in movable]), spare
        for i in movable:
            extra = min(limit - holding[i], max(1, remaining * weights[i] // mass), spare)
            holding[i] = holding[i] + extra
            spare = spare - extra
    return np.array([limit] + holding)


def uneven_parts(rng, count, total, limit, lean):
    if count == 2:
        one = jax.random.randint(rng, (), max(1, total - limit), min(limit, total - 1) + 1)
        return jnp.stack([one, total - one])
    tallies = jnp.asarray(split_up(count, total, limit, lean), jnp.int32)
    pairs = (count - 1) // 2
    giver, sink = tallies[1:1 + 2 * pairs:2], tallies[2:2 + 2 * pairs:2]
    slack = jnp.minimum(giver - 1, limit - sink)
    moved = jax.random.randint(jax.random.fold_in(rng, 1), (pairs,), 0, 1 << 20) % (slack + 1)
    tallies = tallies.at[1:1 + 2 * pairs:2].set(giver - moved).at[2:2 + 2 * pairs:2].set(sink + moved)
    return tallies[jax.random.permutation(jax.random.fold_in(rng, 2), count)]


def noise(stream_key, shape, deviation, limit, kind=jnp.bfloat16):
    entries = jax.random.normal(stream_key, shape, jnp.float32) * deviation
    return jnp.minimum(jnp.maximum(entries, -limit), limit).astype(kind)


def setup_inputs(seed: int = 0) -> dict:
    streams_of = jax.random.split(jax.random.key(seed), 7)
    return {
        "cells": draw_cells(jax.random.fold_in(streams_of[6], 71), 0),
        "w_cell": noise(streams_of[1], (WIDTH, WIDTH), WIDTH ** -0.5, 0.21875),
        "w_mix": noise(streams_of[2], (WIDTH, WIDTH), WIDTH ** -0.5, 0.21875),
        "w_pool": noise(streams_of[3], (WIDTH, WIDTH), WIDTH ** -0.5, 0.21875),
        "pairs": draw_pairs(jax.random.fold_in(streams_of[6], 71), 0),
        "counts": uneven_parts(streams_of[5], READERS, READERS * PAIR_DEV * 3 // 4, PAIR_DEV, 2).astype(jnp.int32),
    }


SOFTMAX_WARMTH = 0.07
EPSILON = 1e-06

def pair_scores(left_block, right_block, w_mix, w_pool):
    left_wide = left_block.astype(jnp.float32)
    right_wide = right_block.astype(jnp.float32)
    score_scale = 1.0 / math.sqrt(left_block.shape[2])
    forward = jnp.einsum('psd,ptd->pst', left_wide, right_wide) * score_scale
    backward = jnp.einsum('ptd,psd->pts', right_wide, left_wide) * score_scale
    attend_left_side = jax.nn.softmax(forward, axis=-1).astype(jnp.bfloat16)
    attend_right = jax.nn.softmax(backward, axis=-1).astype(jnp.bfloat16)
    context_left = jnp.einsum('pst,ptd->psd', attend_left_side.astype(jnp.float32), right_wide)
    context_right = jnp.einsum('pts,psd->ptd', attend_right.astype(jnp.float32), left_wide)
    mixed_left = (left_wide + context_left).astype(jnp.bfloat16)
    mixed_right = (right_wide + context_right).astype(jnp.bfloat16)
    mix_wide = w_mix.astype(jnp.float32)
    pooled_left = lax.optimization_barrier(jnp.mean(jnp.tanh(jnp.einsum('psd,de->pse', mixed_left.astype(jnp.float32), mix_wide)), axis=1)).astype(jnp.bfloat16)
    pooled_right = lax.optimization_barrier(jnp.mean(jnp.tanh(jnp.einsum('psd,de->pse', mixed_right.astype(jnp.float32), mix_wide)), axis=1)).astype(jnp.bfloat16)
    z_left = jnp.dot(pooled_left, w_pool, preferred_element_type=jnp.float32)
    z_right = jnp.dot(pooled_right, w_pool, preferred_element_type=jnp.float32)
    inner_product = lax.optimization_barrier(jnp.mean(z_left * z_right, axis=-1))
    vector_norms = (lax.optimization_barrier(jnp.mean(z_left * z_left, axis=-1)) + EPSILON) * (lax.optimization_barrier(jnp.mean(z_right * z_right, axis=-1)) + EPSILON)
    return inner_product / jnp.sqrt(vector_norms) / SOFTMAX_WARMTH

def reference(cells, w_cell, w_mix, w_pool, pairs, counts):
    projected = jnp.dot(cells.reshape(COLS * SAMPLES, WIDTH), w_cell, preferred_element_type=jnp.float32)
    projected = projected.astype(jnp.bfloat16).reshape(COLS, SAMPLES, WIDTH)
    blocks = pairs.reshape(PAIRS // 8, 8, 2)

    def score_block(block_pairs):
        left_block = jnp.take(projected, block_pairs[:, 0], axis=0)
        right_block = jnp.take(projected, block_pairs[:, 1], axis=0)
        return pair_scores(left_block, right_block, w_mix, w_pool)
    value_rows = lax.map(score_block, blocks).reshape(PAIRS)
    slot_ids = jnp.arange(PAIR_DEV).astype(jnp.int32)
    live = (slot_ids[None, :] < counts[:, None]).reshape(PAIRS)
    return jnp.where(live, value_rows, jnp.zeros_like(value_rows))
```

```python
import functools
import math

import jax
import jax.numpy as jnp
from jax import lax
from jax.experimental import pallas as pl
from jax.experimental.pallas import tpu as pltpu
from jax.sharding import PartitionSpec as P

SOFTMAX_WARMTH = 0.07
EPSILON = 1e-06
LANES = 128
UNROLL = 2
F32 = jnp.float32
BF16 = jnp.bfloat16
NT = (((1,), (1,)), ((), ()))
IX, IY, READER, SLOT, VALID, TOTAL = range(6)


def vmem():
    return pl.BlockSpec(memory_space=pltpu.VMEM)


def smem():
    return pl.BlockSpec(memory_space=pltpu.SMEM)


def dot(a, b):
    return jnp.dot(a, b, preferred_element_type=F32)


def dot_nt(a, b):
    return lax.dot_general(a, b, NT, preferred_element_type=F32)


def project_into(rows, w_cell, w_mix, cells_ref, proj_ref, mixed_ref, base):
    columns, samples, width = cells_ref.shape

    def step(i, carry):
        block = cells_ref[pl.ds(i * rows, rows)].reshape(rows * samples, width)
        proj = dot(block, w_cell[...]).astype(BF16)
        proj_ref[pl.ds(base + i * rows, rows)] = proj.reshape(rows, samples, width)
        mixed = dot(proj, w_mix[...]).astype(BF16)
        mixed_ref[pl.ds(base + i * rows, rows)] = mixed.reshape(rows, samples, width)
        return carry

    lax.fori_loop(0, columns // rows, step, 0)


def project_kernel(own_ref, partner_ref, w_cell, w_mix, proj_ref, mixed_ref):
    columns = own_ref.shape[0]
    rows = 4 if columns % 4 == 0 else 1
    project_into(rows, w_cell, w_mix, own_ref, proj_ref, mixed_ref, 0)
    project_into(rows, w_cell, w_mix, partner_ref, proj_ref, mixed_ref, columns)


def attend_pair(left, right, left_mix, right_mix, score_scale):
    samples = left.shape[0]
    both = jnp.concatenate([dot_nt(right, left), dot_nt(left, right)], axis=1) * score_scale
    weights = jnp.exp(both - jnp.max(both, axis=0, keepdims=True))
    weights = weights * (1.0 / jnp.sum(weights, axis=0, keepdims=True))
    attend = jnp.transpose(weights).astype(BF16)
    mixed_left = left_mix.astype(F32) + dot(attend[:samples], right_mix)
    mixed_right = right_mix.astype(F32) + dot(attend[samples:], left_mix)
    inverse = 1.0 / samples
    return (
        jnp.sum(jnp.tanh(mixed_left), axis=0, keepdims=True) * inverse,
        jnp.sum(jnp.tanh(mixed_right), axis=0, keepdims=True) * inverse,
    )


def score_list(index, rows, x, y, pooled, w_pool, score_scale, out_ref):
    x_proj, x_mix = x
    y_proj, y_mix = y
    pool_x, pool_y = pooled
    total = index[TOTAL, 0]
    capacity = index.shape[1]
    block = min(64, capacity)

    def step(i, carry):
        for u in range(UNROLL):
            at = i * UNROLL + u
            ix, iy = index[IX, at], index[IY, at]
            row_x, row_y = attend_pair(x_proj[ix], y_proj[iy], x_mix[ix], y_mix[iy], score_scale)
            pool_x[pl.ds(at, 1)] = row_x
            pool_y[pl.ds(at, 1)] = row_y
        return carry

    lax.fori_loop(0, (total + UNROLL - 1) // UNROLL, step, 0)

    for start in range(0, capacity, block):

        @pl.when(total > start)
        def _():
            both = jnp.concatenate(
                [pool_x[start : start + block], pool_y[start : start + block]], axis=0
            ).astype(BF16)
            z = dot(both, w_pool[...])
            zx, zy = z[:block], z[block:]
            inner = jnp.mean(zx * zy, axis=1, keepdims=True)
            norms = (jnp.mean(zx * zx, axis=1, keepdims=True) + EPSILON) * (
                jnp.mean(zy * zy, axis=1, keepdims=True) + EPSILON
            )
            score = inner / jnp.sqrt(norms) / SOFTMAX_WARMTH
            score = jnp.transpose(jnp.broadcast_to(score, (block, LANES)))[:1]
            here = rows[:, start : start + block]
            live = here[VALID : VALID + 1] > 0
            score = jnp.where(live, score, 0.0)
            readers, slots = out_ref.shape
            of_reader = here[READER : READER + 1] == lax.broadcasted_iota(
                jnp.int32, (readers, block), 0
            )
            of_slot = here[SLOT : SLOT + 1] == lax.broadcasted_iota(jnp.int32, (slots, block), 0)
            out_ref[...] += lax.dot_general(
                jnp.where(of_reader, score, 0.0),
                of_slot.astype(F32),
                NT,
                preferred_element_type=F32,
                precision=lax.Precision.HIGHEST,
            )


def round_kernel(kinds, score_scale, *refs):
    count = len(kinds)
    index, rows = refs[:count], refs[count : 2 * count]
    (remote, w_cell, w_mix, w_pool, proj, mixed, before, out, r_proj, r_mix, pool_x, pool_y) = refs[
        2 * count :
    ]
    out[...] = before[...]
    columns = remote.shape[0]
    project_into(columns if columns <= 4 else 1, w_cell, w_mix, remote, r_proj, r_mix, 0)
    own, far = (proj, mixed), (r_proj, r_mix)
    for kind, index_ref, rows_ref in zip(kinds, index, rows):
        score_list(
            index_ref,
            rows_ref,
            own,
            far if kind == "far" else own,
            (pool_x, pool_y),
            w_pool,
            score_scale,
            out,
        )


def route_kernel(sizes, whose, ids_ref, out_ref):
    lines, shards, per_shard, pair_dev = sizes
    total_columns = shards * per_shard
    chip_columns = 2 * per_shard
    chips = shards // 2
    quarter = per_shard // lines
    line = lax.axis_index("grp")
    shard = lax.axis_index("shard")
    chip, core = shard // 2, lax.rem(shard, 2)
    readers = ids_ref.shape[0]
    ids = ids_ref[...]
    live = ids >= 0
    kept = jnp.maximum(ids, 0)
    a = kept // total_columns
    b = kept - a * total_columns
    b_chip = b // chip_columns
    b_shard = b // per_shard
    a_local = lax.rem(a, per_shard)
    b_local = lax.rem(b, per_shard)
    reader_row = lax.broadcasted_iota(jnp.int32, ids.shape, 0)
    reader_core = lax.rem(reader_row, 2)
    reader_line = lax.rem(line + reader_row // 2, lines)
    reader_shard = chip * 2 + lax.rem(core + reader_core, 2)
    reader_id = reader_line * shards + reader_shard
    slot = lax.broadcasted_iota(jnp.int32, ids.shape, 1)
    a_own = a_local + per_shard * reader_core
    b_own = b_local + per_shard * lax.rem(b_shard + core, 2)
    upper = (
        lax.broadcasted_iota(jnp.int32, (pair_dev, pair_dev), 0)
        < lax.broadcasted_iota(jnp.int32, (pair_dev, pair_dev), 1)
    ).astype(BF16)
    earlier = (
        lax.broadcasted_iota(jnp.int32, (readers, readers), 1)
        < lax.broadcasted_iota(jnp.int32, (readers, readers), 0)
    ).astype(BF16)
    lanes = out_ref.shape[2]
    place = lax.broadcasted_iota(jnp.int32, (lanes, pair_dev), 0)
    field = lax.broadcasted_iota(jnp.int32, (8, pair_dev), 0)
    for number, (kind, offset) in enumerate(whose):
        if kind == "own":
            mine = live & (reader_row == 0) & (b_chip == chip)
            ix, iy = a_own, b_own
        elif kind == "receive":
            source = ring_place(chip, chips, offset)
            mine = live & (b_shard == source * 2 + core) & (b_local // quarter == line)
            ix, iy = a_own, b_local - line * quarter
        else:
            target = ring_place(chip, chips, -offset)
            mine = live & (reader_core == 0) & (b_chip == target) & (a_local // quarter == line)
            ix, iy = b_own, a_local - line * quarter
        taken = mine.astype(BF16)
        before = dot(taken, upper)
        row_total = jnp.sum(mine.astype(F32), axis=1, keepdims=True)
        offsets = dot(earlier, row_total.astype(BF16))
        position = (before + offsets).astype(jnp.int32)
        position = jnp.where(mine, position, -1)
        total = jnp.sum(row_total, axis=0, keepdims=True)
        packed = jnp.zeros((8, lanes), F32)
        for r in range(readers):
            chosen = (place == position[r : r + 1]).astype(BF16)
            fields = jnp.where(field == VALID, 1, 0)
            for which, value in ((IX, ix), (IY, iy), (READER, reader_id), (SLOT, slot)):
                fields = jnp.where(field == which, value[r : r + 1], fields)
            packed = packed + dot_nt(fields.astype(BF16), chosen)
        row = lax.broadcasted_iota(jnp.int32, (8, lanes), 0)
        packed = jnp.where(row == TOTAL, total, packed)
        out_ref[number] = packed.astype(jnp.int32)


def ring_place(chip, chips, offset):
    half = chips // 2
    place = jnp.where(chip < half, 2 * chip, 2 * (chip - half) + 1)
    other = lax.rem(place + offset + 2 * chips, chips)
    return other // 2 + half * lax.rem(other, 2)


def ring_of(chips):
    half = chips // 2
    return [p // 2 + half * (p % 2) for p in range(chips)]


def local(mesh_shape, cells, w_cell, w_mix, w_pool, pairs, counts):
    lines, shards = mesh_shape["grp"], mesh_shape["shard"]
    chips = shards // 2
    per_shard, samples, width = cells.shape
    pair_dev = pairs.shape[0]
    quarter = per_shard // lines
    line = lax.axis_index("grp")
    score_scale = 1.0 / math.sqrt(width)
    ring = ring_of(chips)

    def from_ahead(offset):
        return [
            (2 * ring[(p + offset) % chips] + c, 2 * ring[p] + c) for p in range(chips) for c in (0, 1)
        ]

    offsets = range(1, chips // 2 + 1)
    swap = [(s, s ^ 1) for s in range(shards)]
    partner = lax.ppermute(cells, "shard", swap)
    share = lax.dynamic_slice_in_dim(cells, line * quarter, quarter, 0)
    remote = [lax.ppermute(share, "shard", from_ahead(d)) for d in offsets]

    slot = jnp.arange(pair_dev, dtype=jnp.int32)
    ids = jnp.where(slot < counts[0], pairs[:, 0] * (shards * per_shard) + pairs[:, 1], -1)
    ids = jnp.stack([ids, lax.ppermute(ids, "shard", swap)])
    ids = jnp.concatenate(
        [ids]
        + [
            lax.ppermute(ids, "grp", [((g + k) % lines, g) for g in range(lines)])
            for k in range(1, lines)
        ]
    )

    two_sided = [d for d in offsets if 2 * d != chips]
    whose = (
        [("own", 0)]
        + [("receive", d) for d in offsets]
        + [("send", d) for d in two_sided]
    )
    most = 2 * lines * min(pair_dev, 2 * pair_dev // shards)
    lanes = -(-max(most, pair_dev) // LANES) * LANES
    lists = pl.pallas_call(
        functools.partial(route_kernel, (lines, shards, per_shard, pair_dev), whose),
        out_shape=jax.ShapeDtypeStruct((len(whose), 8, lanes), jnp.int32),
        in_specs=[vmem()],
        out_specs=vmem(),
        name="route",
    )(ids)
    received = {
        d: lax.ppermute(lists[1 + len(offsets) + i], "shard", from_ahead(d))
        for i, d in enumerate(two_sided)
    }

    block = jax.ShapeDtypeStruct((2 * per_shard, samples, width), BF16)
    proj, mixed = pl.pallas_call(
        project_kernel,
        out_shape=(block, block),
        in_specs=[vmem()] * 4,
        out_specs=(vmem(), vmem()),
        compiler_params=pltpu.CompilerParams(vmem_limit_bytes=32 * 2**20),
        name="project",
    )(cells, partner, w_cell, w_mix)

    out = jnp.zeros((lines * shards, pair_dev), F32)
    order = sorted(offsets, reverse=True)
    for d in order:
        use = [lists[d]]
        kinds = ["far"]
        if d in received:
            use.append(received[d])
            kinds.append("far")
        if d == order[0]:
            use.append(lists[0])
            kinds.append("own")
        out = pl.pallas_call(
            functools.partial(round_kernel, tuple(kinds), score_scale),
            out_shape=jax.ShapeDtypeStruct(out.shape, F32),
            in_specs=[smem()] * len(use) + [vmem()] * (len(use) + 7),
            out_specs=vmem(),
            scratch_shapes=[
                pltpu.VMEM((quarter, samples, width), BF16),
                pltpu.VMEM((quarter, samples, width), BF16),
                pltpu.VMEM((lanes, width), F32),
                pltpu.VMEM((lanes, width), F32),
            ],
            compiler_params=pltpu.CompilerParams(vmem_limit_bytes=40 * 2**20),
            name=f"round{d}",
        )(*use, *use, remote[d - 1], w_cell, w_mix, w_pool, proj, mixed, out)

    back = lax.all_to_all(out, ("grp", "shard"), 0, 0, tiled=True)
    return jnp.sum(back, axis=0)


def solution(mesh):
    placed = (P("shard", None, None), P(), P(), P(), P(("grp", "shard"), None), P(("grp", "shard")))
    return jax.shard_map(
        functools.partial(local, dict(mesh.shape)),
        mesh=mesh,
        in_specs=placed,
        out_specs=P(("grp", "shard")),
        check_vma=False,
    )
```

```python
import functools
import math

import jax
import jax.numpy as jnp
from jax import lax
from jax.experimental import pallas as pl
from jax.experimental.pallas import tpu as pltpu
from jax.sharding import PartitionSpec as P

SOFTMAX_WARMTH = 0.07
EPSILON = 1e-06
LANES = 128
UNROLL = 8
F32 = jnp.float32
BF16 = jnp.bfloat16
NT = (((1,), (1,)), ((), ()))
IX, IY, READER, SLOT, VALID, TOTAL = range(6)


def vmem():
    return pl.BlockSpec(memory_space=pltpu.VMEM)


def hbm():
    return pl.BlockSpec(memory_space=pltpu.HBM)


def in_hbm(x):
    return pltpu.with_memory_space_constraint(x, pltpu.HBM)


def smem():
    return pl.BlockSpec(memory_space=pltpu.SMEM)


def dot(a, b):
    return jnp.dot(a, b, preferred_element_type=F32)


def dot_nt(a, b):
    return lax.dot_general(a, b, NT, preferred_element_type=F32)


def project_columns(block, w_cell, w_mix, proj_ref, mixed_ref, at):
    columns, samples, width = block.shape
    proj = dot(block.reshape(columns * samples, width), w_cell[...]).astype(BF16)
    proj_ref[at : at + columns] = proj.reshape(block.shape)
    mixed_ref[at : at + columns] = dot(proj, w_mix[...]).astype(BF16).reshape(block.shape)


def project_kernel(own, partner, w_cell, w_mix, proj, mixed, own_in, cell_in, mix_in, sems):
    columns = own.shape[0]
    half = columns // 2
    copies = [
        pltpu.make_async_copy(w_cell, cell_in, sems.at[0]),
        pltpu.make_async_copy(own.at[:half], own_in.at[:half], sems.at[1]),
        pltpu.make_async_copy(w_mix, mix_in, sems.at[2]),
        pltpu.make_async_copy(own.at[half:], own_in.at[half:], sems.at[3]),
    ]
    for copy in copies:
        copy.start()
    for copy in copies[:3]:
        copy.wait()
    project_columns(own_in[:half], cell_in, mix_in, proj, mixed, 0)
    copies[3].wait()
    project_columns(own_in[half:], cell_in, mix_in, proj, mixed, half)
    project_columns(partner[...], cell_in, mix_in, proj, mixed, columns)


def attend_pairs(pairs, proj, mixed, score_scale):
    samples = proj.shape[1]
    inverse = 1.0 / samples
    lane = lax.broadcasted_iota(jnp.int32, (samples, 2 * samples), 1)
    weights = []
    for x, y in pairs:
        left, right = proj[x], proj[y]
        both = dot_nt(
            jnp.concatenate([right, left], axis=0), jnp.concatenate([left, right], axis=0)
        )
        weights.append(jnp.where(lane < samples, both[:samples], both[samples:]) * score_scale)
    weights = [jnp.exp(w - jnp.max(w, axis=0, keepdims=True)) for w in weights]
    weights = [w * (1.0 / jnp.sum(w, axis=0, keepdims=True)) for w in weights]
    attend = [jnp.transpose(w).astype(BF16) for w in weights]
    context = [
        (dot(t[:samples], mixed[y]), dot(t[samples:], mixed[x])) for t, (x, y) in zip(attend, pairs)
    ]
    return [
        [
            jnp.sum(jnp.tanh(mixed[c].astype(F32) + add), axis=0, keepdims=True) * inverse
            for c, add in zip(pair, adds)
        ]
        for pair, adds in zip(pairs, context)
    ]


def round_kernel(count, base, score_scale, *refs):
    index, rows = refs[:count], refs[count : 2 * count]
    remote, w_cell, w_mix, w_pool, _, _, *before = refs[2 * count : -6]
    proj, mixed, out, pool_x, pool_y, fields = refs[-6:]
    project_columns(remote[...], w_cell, w_mix, proj, mixed, base)
    lanes = index[0].shape[1]
    starts = [0]
    for ref in index:
        starts.append(starts[-1] + ref[TOTAL, 0])
    total = starts[-1]

    def column(at):
        x, y = index[0][IX, jnp.minimum(at, lanes - 1)], index[0][IY, jnp.minimum(at, lanes - 1)]
        for ref, start in zip(index[1:], starts[1:]):
            here = jnp.clip(at - start, 0, lanes - 1)
            x = jnp.where(at >= start, ref[IX, here], x)
            y = jnp.where(at >= start, ref[IY, here], y)
        return x, y

    def step(i, carry):
        pairs = [column(i * UNROLL + u) for u in range(UNROLL)]
        for u, (row_x, row_y) in enumerate(attend_pairs(pairs, proj, mixed, score_scale)):
            pool_x[pl.ds(i * UNROLL + u, 1)] = row_x
            pool_y[pl.ds(i * UNROLL + u, 1)] = row_y
        return carry

    lax.fori_loop(0, (total + UNROLL - 1) // UNROLL, step, 0)

    capacity = fields.shape[1]
    lane = lax.broadcasted_iota(jnp.int32, fields.shape, 1)
    joined = jnp.zeros(fields.shape, jnp.int32)
    for ref, start in zip(rows, starts):
        wide = [ref[...]] + [jnp.zeros((8, lanes), jnp.int32)] * (count - 1)
        wide = jnp.concatenate(wide, axis=1) if count > 1 else wide[0]
        joined = jnp.where(lane >= start, pltpu.roll(wide, start, 1), joined)
    fields[...] = joined
    out[...] = before[0][...] if before else jnp.zeros(out.shape, F32)
    block = LANES
    readers, slots = out.shape
    for start in range(0, capacity, block):

        @pl.when(total > start)
        def _():
            both = jnp.concatenate(
                [pool_x[start : start + block], pool_y[start : start + block]], axis=0
            ).astype(BF16)
            z = dot(both, w_pool[...])
            zx, zy = z[:block], z[block:]
            inner = jnp.mean(zx * zy, axis=1, keepdims=True)
            norms = (jnp.mean(zx * zx, axis=1, keepdims=True) + EPSILON) * (
                jnp.mean(zy * zy, axis=1, keepdims=True) + EPSILON
            )
            score = inner / jnp.sqrt(norms) / SOFTMAX_WARMTH
            score = jnp.transpose(jnp.broadcast_to(score, (block, block)))[:1]
            here = fields[:, start : start + block]
            live = (here[VALID : VALID + 1] > 0) & (
                lax.broadcasted_iota(jnp.int32, (1, block), 1) < total - start
            )
            score = jnp.where(live, score, 0.0)
            of_reader = here[READER : READER + 1] == lax.broadcasted_iota(
                jnp.int32, (readers, block), 0
            )
            of_slot = here[SLOT : SLOT + 1] == lax.broadcasted_iota(jnp.int32, (slots, block), 0)
            out[...] += lax.dot_general(
                jnp.where(of_reader, score, 0.0),
                of_slot.astype(F32),
                NT,
                preferred_element_type=F32,
                precision=lax.Precision.HIGHEST,
            )


def prepare_kernel(total_columns, quarter, cells, pairs, counts, share, ids, held, sems):
    first = lax.axis_index("grp") * quarter
    copy = pltpu.make_async_copy(cells.at[pl.ds(first, quarter)], share, sems.at[0])
    copy.start()
    copy_pairs = pltpu.make_async_copy(pairs, held, sems.at[1])
    copy_pairs.start()
    copy_pairs.wait()
    slot = lax.broadcasted_iota(jnp.int32, ids.shape, 1)
    ids[...] = jnp.where(slot < counts[0], held[:1] * total_columns + held[1:], -1)
    copy.wait()


def route_kernel(sizes, whose, *refs):
    lines, shards, per_shard, pair_dev = sizes
    ids_refs, out_refs = refs[:lines], refs[lines + 1 :]
    total_columns = shards * per_shard
    chip_columns = 2 * per_shard
    chips = shards // 2
    quarter = per_shard // lines
    line = lax.axis_index("grp")
    shard = lax.axis_index("shard")
    chip, core = shard // 2, lax.rem(shard, 2)
    ids = jnp.concatenate([ref[...] for ref in ids_refs], axis=0)
    live = ids >= 0
    kept = jnp.maximum(ids, 0)
    a = kept // total_columns
    b = kept - a * total_columns
    b_chip = b // chip_columns
    b_shard = b // per_shard
    a_local = lax.rem(a, per_shard)
    b_local = lax.rem(b, per_shard)
    reader_row = lax.broadcasted_iota(jnp.int32, ids.shape, 0)
    reader_id = lax.rem(line + reader_row, lines) * shards + shard
    slot = lax.broadcasted_iota(jnp.int32, ids.shape, 1)
    b_own = b_local + per_shard * lax.rem(b_shard + core, 2)
    upper = (
        lax.broadcasted_iota(jnp.int32, (pair_dev, pair_dev), 0)
        < lax.broadcasted_iota(jnp.int32, (pair_dev, pair_dev), 1)
    ).astype(BF16)
    lanes = out_refs[0].shape[1]
    place = lax.broadcasted_iota(jnp.int32, (lanes, pair_dev), 0)
    field = lax.broadcasted_iota(jnp.int32, (8, pair_dev), 0)
    for (kind, offset), out_ref in zip(whose, out_refs):
        base = chip_columns + (offset - 1) * quarter
        if kind == "own":
            mine = live & (reader_row == 0) & (b_chip == chip)
            ix, iy = a_local, b_own
        elif kind in ("receive", "partner"):
            here = core if kind == "receive" else 1 - core
            source = ring_place(chip, chips, offset)
            mine = live & (b_shard == source * 2 + here) & (b_local // quarter == line)
            ix = a_local if kind == "receive" else a_local + per_shard
            iy = base + b_local - line * quarter
        else:
            target = ring_place(chip, chips, -offset)
            mine = live & (b_chip == target) & (a_local // quarter == line)
            ix, iy = b_own, base + a_local - line * quarter
        before = dot(mine.astype(BF16), upper)
        row_total = jnp.sum(mine.astype(F32), axis=1, keepdims=True)
        total = jnp.zeros((1, 1), F32)
        packed = jnp.zeros((8, lanes), F32)
        for r in range(lines if kind != "own" else 1):
            position = (before[r : r + 1] + total).astype(jnp.int32)
            position = jnp.where(mine[r : r + 1], position, -1)
            total = total + row_total[r : r + 1]
            chosen = (place == position).astype(BF16)
            fields = jnp.where(field == VALID, 1, 0)
            for which, value in ((IX, ix), (IY, iy), (READER, reader_id), (SLOT, slot)):
                fields = jnp.where(field == which, value[r : r + 1], fields)
            packed = packed + dot_nt(fields.astype(BF16), chosen)
        row = lax.broadcasted_iota(jnp.int32, (8, lanes), 0)
        out_ref[...] = jnp.where(row == TOTAL, total, packed).astype(jnp.int32)


def ring_place(chip, chips, offset):
    half = chips // 2
    place = jnp.where(chip < half, 2 * chip, 2 * (chip - half) + 1)
    other = lax.rem(place + offset + 2 * chips, chips)
    return other // 2 + half * lax.rem(other, 2)


def ring_of(chips):
    half = chips // 2
    return [p // 2 + half * (p % 2) for p in range(chips)]


def local(mesh_shape, cells, w_cell, w_mix, w_pool, pairs, counts):
    lines, shards = mesh_shape["grp"], mesh_shape["shard"]
    chips = shards // 2
    per_shard, samples, width = cells.shape
    pair_dev = pairs.shape[0]
    quarter = per_shard // lines
    score_scale = 1.0 / math.sqrt(width)
    ring = ring_of(chips)

    def from_ahead(offset):
        return [
            (2 * ring[(p + offset) % chips] + c, 2 * ring[p] + c) for p in range(chips) for c in (0, 1)
        ]

    offsets = range(1, chips // 2 + 1)
    swap = [(s, s ^ 1) for s in range(shards)]
    partner = lax.ppermute(cells, "shard", swap)
    share, ids = pl.pallas_call(
        functools.partial(prepare_kernel, shards * per_shard, quarter),
        out_shape=(
            jax.ShapeDtypeStruct((quarter, samples, width), BF16),
            jax.ShapeDtypeStruct((1, pair_dev), jnp.int32),
        ),
        in_specs=[hbm(), hbm(), smem()],
        out_specs=(vmem(), vmem()),
        scratch_shapes=[pltpu.VMEM((2, pair_dev), jnp.int32), pltpu.SemaphoreType.DMA((2,))],
        compiler_params=pltpu.CompilerParams(vmem_limit_bytes=4 * 2**20),
        name="prepare",
    )(in_hbm(cells), in_hbm(pairs.T), counts)
    remote = [lax.ppermute(share, "shard", from_ahead(d)) for d in offsets]
    ids = [ids] + [
        lax.ppermute(ids, "grp", [((g + k) % lines, g) for g in range(lines)])
        for k in range(1, lines)
    ]

    store = jax.ShapeDtypeStruct((2 * per_shard + len(offsets) * quarter, samples, width), BF16)
    store_bytes = 2 * math.prod(store.shape)
    weight_bytes = 2 * width * width
    proj, mixed = pl.pallas_call(
        project_kernel,
        out_shape=(store, store),
        in_specs=[hbm(), vmem(), hbm(), hbm()],
        out_specs=(vmem(), vmem()),
        scratch_shapes=[
            pltpu.VMEM(cells.shape, BF16),
            pltpu.VMEM(w_cell.shape, BF16),
            pltpu.VMEM(w_mix.shape, BF16),
            pltpu.SemaphoreType.DMA((4,)),
        ],
        compiler_params=pltpu.CompilerParams(
            vmem_limit_bytes=2 * store_bytes + 2 * weight_bytes + 16 * 2**20
        ),
        name="project",
    )(in_hbm(cells), pltpu.with_memory_space_constraint(partner, pltpu.VMEM), in_hbm(w_cell), in_hbm(w_mix))

    two_sided = [d for d in offsets if 2 * d != chips]
    whose = (
        [("own", 0)]
        + [("receive", d) for d in offsets]
        + [("partner", d) for d in offsets]
        + [("send", d) for d in two_sided]
    )
    most = lines * min(pair_dev, 4 * pair_dev // shards)
    lanes = -(-max(most, pair_dev) // LANES) * LANES
    lists = pl.pallas_call(
        functools.partial(route_kernel, (lines, shards, per_shard, pair_dev), whose),
        out_shape=[jax.ShapeDtypeStruct((8, lanes), jnp.int32)] * len(whose),
        in_specs=[vmem()] * lines + [pl.BlockSpec(memory_space=pl.ANY)],
        out_specs=[vmem()] * len(whose),
        compiler_params=pltpu.CompilerParams(vmem_limit_bytes=4 * 2**20),
        name="route",
    )(*ids, proj)
    lists = dict(zip(whose, lists))
    in_round = {d: [lists["receive", d]] for d in offsets}
    in_round[offsets[-1]].append(lists["own", 0])
    for d in offsets:
        in_round[d].append(lax.ppermute(lists["partner", d], "shard", swap))
    for d in two_sided:
        in_round[d].append(lax.ppermute(lists["send", d], "shard", from_ahead(d)))

    out = []
    for d in reversed(offsets):
        use = in_round[d]
        count = len(use)
        proj, mixed, *out = pl.pallas_call(
            functools.partial(
                round_kernel, count, 2 * per_shard + (d - 1) * quarter, score_scale
            ),
            out_shape=(store, store, jax.ShapeDtypeStruct((lines * shards, pair_dev), F32)),
            in_specs=[smem()] * count + [vmem()] * (count + 6 + len(out)),
            out_specs=(vmem(),) * 3,
            input_output_aliases={2 * count + 4 + i: i for i in range(2 + len(out))},
            scratch_shapes=[
                pltpu.VMEM((count * lanes, width), F32),
                pltpu.VMEM((count * lanes, width), F32),
                pltpu.VMEM((8, count * lanes), jnp.int32),
            ],
            compiler_params=pltpu.CompilerParams(
                vmem_limit_bytes=2 * store_bytes + 4 * weight_bytes + 12 * 2**20
            ),
            name=f"round{d}",
        )(*use, *use, remote[d - 1], w_cell, w_mix, w_pool, proj, mixed, *out)
    (out,) = out

    back = lax.all_to_all(out, ("grp", "shard"), 0, 0, tiled=True)
    return jnp.sum(back, axis=0)


def solution(mesh):
    placed = (P("shard", None, None), P(), P(), P(), P(("grp", "shard"), None), P(("grp", "shard")))
    return jax.shard_map(
        functools.partial(local, dict(mesh.shape)),
        mesh=mesh,
        in_specs=placed,
        out_specs=P(("grp", "shard")),
        check_vma=False,
    )
```

```python
import functools
import math

import jax
import jax.numpy as jnp
from jax import lax
from jax.experimental import pallas as pl
from jax.experimental.pallas import tpu as pltpu
from jax.sharding import PartitionSpec as P

SOFTMAX_WARMTH = 0.07
EPSILON = 1e-06
LANES = 128
STEPS = (16, 8, 4)
F32 = jnp.float32
BF16 = jnp.bfloat16
NT = (((1,), (1,)), ((), ()))
IX, IY, READER, SLOT, VALID, TOTAL = range(6)


def vmem():
    return pl.BlockSpec(memory_space=pltpu.VMEM)


def hbm():
    return pl.BlockSpec(memory_space=pltpu.HBM)


def in_hbm(x):
    return pltpu.with_memory_space_constraint(x, pltpu.HBM)


def smem():
    return pl.BlockSpec(memory_space=pltpu.SMEM)


def dot(a, b):
    return jnp.dot(a, b, preferred_element_type=F32)


def dot_nt(a, b):
    return lax.dot_general(a, b, NT, preferred_element_type=F32)


def first_projection(blocks, w_cell, proj, at):
    _, samples, width = blocks[0].shape
    cells = jnp.concatenate([block.reshape(-1, width) for block in blocks], axis=0)
    rows = dot(cells, w_cell[...]).astype(BF16)
    proj[at : at + rows.shape[0] // samples] = rows.reshape(-1, samples, width)
    return rows


def second_projection(rows, w_mix, mixed, at):
    _, samples, width = mixed.shape
    mixed[at : at + rows.shape[0] // samples] = (
        dot(rows, w_mix[...]).astype(BF16).reshape(-1, samples, width)
    )


def project_kernel(own, partner, w_cell, w_mix, w_pool, proj, mixed, mix_in, pool_in, own_in, sems):
    columns = own.shape[0]
    copies = [
        pltpu.make_async_copy(w_mix, mix_in, sems.at[0]),
        pltpu.make_async_copy(own, own_in, sems.at[1]),
        pltpu.make_async_copy(w_pool, pool_in, sems.at[2]),
    ]
    for copy in copies:
        copy.start()
    rows = first_projection([partner[...]], w_cell, proj, columns)
    copies[0].wait()
    second_projection(rows, mix_in, mixed, columns)
    copies[1].wait()
    rows = first_projection([own_in[...]], w_cell, proj, 0)
    second_projection(rows, mix_in, mixed, 0)
    copies[2].wait()


def chip_kernel(score_scale, index, rows, proj, mixed, w_pool, _, out, pool_x, pool_y, fields):
    out[...] = jnp.zeros(out.shape, F32)
    lists = [(index, rows, 0)]
    attend_lists(lists, 0, proj, mixed, score_scale, pool_x, pool_y)
    score_lists(lists, w_pool, out, pool_x, pool_y, fields)


def attend_pairs(pairs, proj, mixed, score_scale):
    samples = proj.shape[1]
    shape = (samples, 2 * samples)
    lane = lax.broadcasted_iota(jnp.int32, shape, 1)
    first = lane < samples
    unit = (lax.rem(lane, samples) == lax.broadcasted_iota(jnp.int32, shape, 0)).astype(F32)
    weights = []
    for x, y in pairs:
        both = dot_nt(
            jnp.concatenate([proj[y], proj[x]], axis=0), jnp.concatenate([proj[x], proj[y]], axis=0)
        )
        weights.append(jnp.where(first, both[:samples], both[samples:]) * score_scale)
    weights = [jnp.exp(w - jnp.max(w, axis=0, keepdims=True)) for w in weights]
    weights = [w * (1.0 / jnp.sum(w, axis=0, keepdims=True)) for w in weights]
    attend = [
        jnp.transpose(
            jnp.concatenate([jnp.where(first, w, unit), jnp.where(first, unit, w)], axis=0)
        ).astype(BF16)
        for w in weights
    ]
    pooled = []
    for t, (x, y) in zip(attend, pairs):
        rows = jnp.tanh(dot(t, jnp.concatenate([mixed[y], mixed[x]], axis=0)))
        pooled.append(
            [jnp.sum(r, axis=0, keepdims=True) * (1.0 / samples) for r in (rows[:samples], rows[samples:])]
        )
    return pooled


def lists_of(held, index, rows):
    return [(i, r, 8 * at) for i, r, number in zip(index, rows, held) for at in range(number)]


def near_kernel(chips, base, held, score_scale, *refs):
    count = len(held)
    index, remote = refs[:count], refs[count : count + chips]
    w_cell, w_mix, _, _, proj, mixed, pool_x, pool_y = refs[count + chips :]
    rows = first_projection([ref[...] for ref in remote], w_cell, proj, base)
    second_projection(rows, w_mix, mixed, base)
    attend_lists(lists_of(held, index, index), 0, proj, mixed, score_scale, pool_x, pool_y)


def far_kernel(held, near, score_scale, *refs):
    count = len(held)
    index, rows = refs[:count], refs[count : 2 * count]
    proj, mixed, w_pool, before, _, _, out, pool_x, pool_y, fields = refs[2 * count :]
    lists = lists_of(held, index, rows)
    out[...] = before[...]
    attend_lists(lists, near, proj, mixed, score_scale, pool_x, pool_y)
    score_lists(lists, w_pool, out, pool_x, pool_y, fields)


def starts_of(lists):
    starts = [0]
    for ref, _, row in lists:
        starts.append(starts[-1] + ref[row + TOTAL, 0])
    return starts


def attend_lists(lists, done, proj, mixed, score_scale, pool_x, pool_y):
    lanes = lists[0][0].shape[1]
    starts = starts_of(lists)
    todo = list(zip(lists, starts))[done:]

    def column(at):
        x = y = 0
        for (ref, _, row), start in todo:
            here = jnp.clip(at - start, 0, lanes - 1)
            x = jnp.where(at >= start, ref[row + IX, here], x)
            y = jnp.where(at >= start, ref[row + IY, here], y)
        return x, y

    def step(first, size, i, carry):
        at = [first + i * size + u for u in range(size)]
        pooled = attend_pairs([column(p) for p in at], proj, mixed, score_scale)
        for p, (row_x, row_y) in zip(at, pooled):
            pool_x[pl.ds(p, 1)] = row_x
            pool_y[pl.ds(p, 1)] = row_y
        return carry

    large, middle, small = STEPS
    left = starts[-1] - starts[done]
    rest = lax.rem(left, large)
    counts = (
        left // large + (rest > middle + small).astype(jnp.int32),
        ((rest > small) & (rest <= middle + small)).astype(jnp.int32),
        (((rest > 0) & (rest <= small)) | ((rest > middle) & (rest <= middle + small))).astype(jnp.int32),
    )
    first = starts[done]
    for size, count in zip(STEPS, counts):
        lax.fori_loop(0, count, functools.partial(step, first, size), 0)
        first = first + size * count


def score_lists(lists, w_pool, out, pool_x, pool_y, fields):
    starts = starts_of(lists)
    total = starts[-1]
    lanes, capacity = lists[0][0].shape[1], fields.shape[1]
    lane = lax.broadcasted_iota(jnp.int32, fields.shape, 1)
    joined = jnp.zeros(fields.shape, jnp.int32)
    for (_, ref, row), start in zip(lists, starts):
        wide = [ref[row : row + 8]] + [jnp.zeros((8, lanes), jnp.int32)] * (capacity // lanes - 1)
        wide = jnp.concatenate(wide, axis=1) if len(wide) > 1 else wide[0]
        joined = jnp.where(lane >= start, pltpu.roll(wide, start, 1), joined)
    fields[...] = joined
    block = LANES
    readers, slots = out.shape

    def step(i, carry):
        here = pl.ds(pl.multiple_of(i * block, block), block)
        z = dot(jnp.concatenate([pool_x[here], pool_y[here]], axis=0).astype(BF16), w_pool[...])
        zx, zy = z[:block], z[block:]
        inner = jnp.mean(zx * zy, axis=1, keepdims=True)
        norms = (jnp.mean(zx * zx, axis=1, keepdims=True) + EPSILON) * (
            jnp.mean(zy * zy, axis=1, keepdims=True) + EPSILON
        )
        score = inner / jnp.sqrt(norms) / SOFTMAX_WARMTH
        score = jnp.transpose(jnp.broadcast_to(score, (block, block)))[:1]
        field = fields[:, here]
        live = (field[VALID : VALID + 1] > 0) & (
            lax.broadcasted_iota(jnp.int32, (1, block), 1) < total - i * block
        )
        score = jnp.where(live, score, 0.0)
        of_reader = field[READER : READER + 1] == lax.broadcasted_iota(
            jnp.int32, (readers, block), 0
        )
        of_slot = field[SLOT : SLOT + 1] == lax.broadcasted_iota(jnp.int32, (slots, block), 0)
        out[...] += lax.dot_general(
            jnp.where(of_reader, score, 0.0),
            of_slot.astype(F32),
            NT,
            preferred_element_type=F32,
            precision=lax.Precision.HIGHEST,
        )
        return carry

    lax.fori_loop(0, (total + block - 1) // block, step, 0)


def share_kernel(quarter, cells, share, sem):
    first = lax.axis_index("grp") * quarter
    copy = pltpu.make_async_copy(cells.at[pl.ds(first, quarter)], share, sem)
    copy.start()
    copy.wait()


def prepare_kernel(sizes, pairs, counts, w_cell, _, ids, own_list, cell_in, held, sems):
    lines, shards, per_shard, pair_dev = sizes
    line, shard = lax.axis_index("grp"), lax.axis_index("shard")
    copy_cell = pltpu.make_async_copy(w_cell, cell_in, sems.at[0])
    copy_pairs = pltpu.make_async_copy(pairs, held, sems.at[1])
    copy_pairs.start()
    copy_cell.start()
    copy_pairs.wait()
    slot = lax.broadcasted_iota(jnp.int32, ids.shape, 1)
    a, b = held[:1], held[1:]
    live = slot < counts[0]
    ids[...] = jnp.where(live, a * (shards * per_shard) + b, -1)
    mine = live & (b // (2 * per_shard) == shard // 2)
    x = lax.rem(a, per_shard)
    y = lax.rem(b, per_shard) + per_shard * lax.rem(b // per_shard + shard, 2)
    reader = jnp.full_like(slot, line * shards + shard)
    own_list[...] = pack_list(mine, (x, y, reader, slot), own_list.shape[1])
    copy_cell.wait()


def pack_list(mine, values, lanes):
    rows, slots = mine.shape
    earlier = (
        lax.broadcasted_iota(jnp.int32, (slots, slots), 0)
        < lax.broadcasted_iota(jnp.int32, (slots, slots), 1)
    ).astype(BF16)
    place = lax.broadcasted_iota(jnp.int32, (lanes, slots), 0)
    field = lax.broadcasted_iota(jnp.int32, (8, slots), 0)
    before = dot(mine.astype(BF16), earlier)
    row_total = jnp.sum(mine.astype(F32), axis=1, keepdims=True)
    total = jnp.zeros((1, 1), F32)
    packed = jnp.zeros((8, lanes), F32)
    for r in range(rows):
        position = (before[r : r + 1] + total).astype(jnp.int32)
        position = jnp.where(mine[r : r + 1], position, -1)
        total = total + row_total[r : r + 1]
        chosen = (place == position).astype(BF16)
        fields = jnp.where(field == VALID, 1, 0)
        for which, value in zip((IX, IY, READER, SLOT), values):
            fields = jnp.where(field == which, value[r : r + 1], fields)
        packed = packed + dot_nt(fields.astype(BF16), chosen)
    row = lax.broadcasted_iota(jnp.int32, (8, lanes), 0)
    return jnp.where(row == TOTAL, total, packed).astype(jnp.int32)


def route_kernel(sizes, whose, *refs):
    lines, shards, per_shard, pair_dev = sizes
    ids_refs, out_refs = refs[:lines], refs[lines + 1 :]
    total_columns = shards * per_shard
    chip_columns = 2 * per_shard
    chips = shards // 2
    quarter = per_shard // lines
    line = lax.axis_index("grp")
    shard = lax.axis_index("shard")
    chip, core = shard // 2, lax.rem(shard, 2)
    ids = jnp.concatenate([ref[...] for ref in ids_refs], axis=0)
    live = ids >= 0
    kept = jnp.maximum(ids, 0)
    a = kept // total_columns
    b = kept - a * total_columns
    b_chip = b // chip_columns
    b_shard = b // per_shard
    a_local = lax.rem(a, per_shard)
    b_local = lax.rem(b, per_shard)
    reader_row = lax.broadcasted_iota(jnp.int32, ids.shape, 0)
    reader_id = lax.rem(line + reader_row, lines) * shards + shard
    slot = lax.broadcasted_iota(jnp.int32, ids.shape, 1)
    b_own = b_local + per_shard * lax.rem(b_shard + core, 2)
    lanes = out_refs[0].shape[1]
    for group, out_ref in zip(whose, out_refs):
        for at, (kind, offset) in enumerate(group):
            base = chip_columns + (offset - 1) * quarter
            if kind in ("receive", "partner"):
                here = core if kind == "receive" else 1 - core
                source = ring_place(chip, chips, offset)
                mine = live & (b_shard == source * 2 + here) & (b_local // quarter == line)
                x = a_local if kind == "receive" else a_local + per_shard
                y = base + b_local - line * quarter
            else:
                target = ring_place(chip, chips, -offset)
                mine = live & (b_chip == target) & (a_local // quarter == line)
                x, y = b_own, base + a_local - line * quarter
            out_ref[8 * at : 8 * at + 8] = pack_list(mine, (x, y, reader_id, slot), lanes)


def ring_place(chip, chips, offset):
    half = chips // 2
    place = jnp.where(chip < half, 2 * chip, 2 * (chip - half) + 1)
    other = lax.rem(place + offset + 2 * chips, chips)
    return other // 2 + half * lax.rem(other, 2)


def ring_of(chips):
    half = chips // 2
    return [p // 2 + half * (p % 2) for p in range(chips)]


def local(mesh_shape, cells, w_cell, w_mix, w_pool, pairs, counts):
    lines, shards = mesh_shape["grp"], mesh_shape["shard"]
    chips = shards // 2
    per_shard, samples, width = cells.shape
    pair_dev = pairs.shape[0]
    quarter = per_shard // lines
    score_scale = 1.0 / math.sqrt(width)
    ring = ring_of(chips)

    def from_ahead(offset):
        return [
            (2 * ring[(p + offset) % chips] + c, 2 * ring[p] + c) for p in range(chips) for c in (0, 1)
        ]

    offsets = range(1, chips // 2 + 1)
    swap = [(s, s ^ 1) for s in range(shards)]
    sizes = (lines, shards, per_shard, pair_dev)
    most = lines * min(pair_dev, 4 * pair_dev // shards)
    lanes = -(-max(most, pair_dev) // LANES) * LANES
    weight = jax.ShapeDtypeStruct(w_cell.shape, BF16)
    weight_bytes = 2 * width * width
    share = pl.pallas_call(
        functools.partial(share_kernel, quarter),
        out_shape=jax.ShapeDtypeStruct((quarter, samples, width), BF16),
        in_specs=[hbm()],
        out_specs=vmem(),
        scratch_shapes=[pltpu.SemaphoreType.DMA(())],
        compiler_params=pltpu.CompilerParams(vmem_limit_bytes=4 * 2**20),
        name="share",
    )(in_hbm(cells))
    remote = {d: lax.ppermute(share, "shard", from_ahead(d)) for d in offsets}
    cells, _ = lax.optimization_barrier((cells, share))
    partner = lax.ppermute(cells, "shard", swap)
    ids, own_list, w_cell = pl.pallas_call(
        functools.partial(prepare_kernel, sizes),
        out_shape=(
            jax.ShapeDtypeStruct((1, pair_dev), jnp.int32),
            jax.ShapeDtypeStruct((8, lanes), jnp.int32),
            weight,
        ),
        in_specs=[hbm(), smem(), hbm(), pl.BlockSpec(memory_space=pl.ANY)],
        out_specs=[vmem()] * 3,
        scratch_shapes=[pltpu.VMEM((2, pair_dev), jnp.int32), pltpu.SemaphoreType.DMA((2,))],
        compiler_params=pltpu.CompilerParams(vmem_limit_bytes=weight_bytes + 4 * 2**20),
        name="prepare",
    )(in_hbm(pairs.T), counts, in_hbm(w_cell), share)
    ids = [ids] + [
        lax.ppermute(ids, "grp", [((g + k) % lines, g) for g in range(lines)])
        for k in range(1, lines)
    ]

    store = jax.ShapeDtypeStruct((2 * per_shard + len(offsets) * quarter, samples, width), BF16)
    scores = jax.ShapeDtypeStruct((lines * shards, pair_dev), F32)
    store_bytes = 2 * math.prod(store.shape)
    weight_bytes = 2 * width * width

    def pool(count):
        return jax.ShapeDtypeStruct((count * lanes + STEPS[0], width), F32)

    def limit(spare):
        return pltpu.CompilerParams(
            vmem_limit_bytes=2 * store_bytes + 3 * weight_bytes + spare * 2**20
        )

    proj, mixed, w_mix, w_pool = pl.pallas_call(
        project_kernel,
        out_shape=[store, store, weight, weight],
        in_specs=[hbm(), vmem(), vmem(), hbm(), hbm()],
        out_specs=[vmem()] * 4,
        scratch_shapes=[pltpu.VMEM(cells.shape, BF16), pltpu.SemaphoreType.DMA((3,))],
        compiler_params=limit(16),
        name="project",
    )(in_hbm(cells), partner, w_cell, in_hbm(w_mix), in_hbm(w_pool))

    groups = [offsets[i : i + 2] for i in range(0, len(offsets), 2)]
    whose, spans = [], []
    for group in groups:
        near = [[(kind, d) for d in group] for kind in ("receive", "partner")]
        far = [[("send", d)] for d in group if 2 * d != chips]
        spans.append((len(whose), len(whose) + len(near), len(whose) + len(near + far)))
        whose += near + far
    lists = pl.pallas_call(
        functools.partial(route_kernel, sizes, whose),
        out_shape=[jax.ShapeDtypeStruct((8 * len(kinds), lanes), jnp.int32) for kinds in whose],
        in_specs=[vmem()] * lines + [pl.BlockSpec(memory_space=pl.ANY)],
        out_specs=[vmem()] * len(whose),
        compiler_params=pltpu.CompilerParams(vmem_limit_bytes=4 * 2**20),
        name="route",
    )(*ids, proj)
    arrived = []
    for kinds, packed in zip(whose, lists):
        kind, d = kinds[0]
        if kind == "partner":
            packed = lax.ppermute(packed, "shard", swap)
        elif kind == "send":
            packed = lax.ppermute(packed, "shard", from_ahead(d))
        arrived.append(packed)

    out = pl.pallas_call(
        functools.partial(chip_kernel, score_scale),
        out_shape=scores,
        in_specs=[smem()] + [vmem()] * 4 + [pl.BlockSpec(memory_space=pl.ANY)],
        out_specs=vmem(),
        scratch_shapes=[
            pltpu.VMEM(pool(1).shape, F32),
            pltpu.VMEM(pool(1).shape, F32),
            pltpu.VMEM((8, lanes), jnp.int32),
        ],
        compiler_params=limit(16),
        name="chip",
    )(own_list, own_list, proj, mixed, w_pool, lists[-1])

    for group, (first, middle, last) in zip(groups, spans):
        use = arrived[first:last]
        held = [x.shape[0] // 8 for x in use]
        number = middle - first
        at = number + len(group) + 2
        proj, mixed, pool_x, pool_y = pl.pallas_call(
            functools.partial(
                near_kernel,
                len(group),
                2 * per_shard + (group[0] - 1) * quarter,
                held[:number],
                score_scale,
            ),
            out_shape=(store, store, pool(sum(held)), pool(sum(held))),
            in_specs=[smem()] * number + [vmem()] * (len(group) + 4),
            out_specs=[vmem()] * 4,
            input_output_aliases={at: 0, at + 1: 1},
            compiler_params=limit(20),
            name="near" + "_".join(map(str, group)),
        )(*use[:number], *(remote[d] for d in group), w_cell, w_mix, proj, mixed)
        at = 2 * len(use) + 3
        out, *_ = pl.pallas_call(
            functools.partial(far_kernel, held, sum(held[:number]), score_scale),
            out_shape=(scores, pool(sum(held)), pool(sum(held))),
            in_specs=[smem()] * len(use) + [vmem()] * (len(use) + 6),
            out_specs=[vmem()] * 3,
            input_output_aliases={at: 0, at + 1: 1, at + 2: 2},
            scratch_shapes=[pltpu.VMEM((8, sum(held) * lanes), jnp.int32)],
            compiler_params=limit(20),
            name="far" + "_".join(map(str, group)),
        )(*use, *use, proj, mixed, w_pool, out, pool_x, pool_y)

    back = lax.all_to_all(out, ("grp", "shard"), 0, 0, tiled=True)
    return jnp.sum(back, axis=0)


def solution(mesh):
    placed = (P("shard", None, None), P(), P(), P(), P(("grp", "shard"), None), P(("grp", "shard")))
    return jax.shard_map(
        functools.partial(local, dict(mesh.shape)),
        mesh=mesh,
        in_specs=placed,
        out_specs=P(("grp", "shard")),
        check_vma=False,
    )
```

```python
import functools
import math

import jax
import jax.numpy as jnp
from jax import lax
from jax.experimental import pallas as pl
from jax.experimental.pallas import tpu as pltpu
from jax.sharding import PartitionSpec as P

SOFTMAX_WARMTH = 0.07
EPSILON = 1e-06
LANES = 128
STEPS = (16, 8, 4)
F32 = jnp.float32
BF16 = jnp.bfloat16
NT = (((1,), (1,)), ((), ()))
IX, IY, READER, SLOT, VALID, TOTAL = range(6)


def vmem():
    return pl.BlockSpec(memory_space=pltpu.VMEM)


def hbm():
    return pl.BlockSpec(memory_space=pltpu.HBM)


def in_hbm(x):
    return pltpu.with_memory_space_constraint(x, pltpu.HBM)


def smem():
    return pl.BlockSpec(memory_space=pltpu.SMEM)


def dot(a, b):
    return jnp.dot(a, b, preferred_element_type=F32)


def dot_nt(a, b):
    return lax.dot_general(a, b, NT, preferred_element_type=F32)


def first_projection(blocks, w_cell, proj, at):
    _, samples, width = blocks[0].shape
    cells = jnp.concatenate([block.reshape(-1, width) for block in blocks], axis=0)
    rows = dot(cells, w_cell[...]).astype(BF16)
    proj[at : at + rows.shape[0] // samples] = rows.reshape(-1, samples, width)
    return rows


def second_projection(rows, w_mix, mixed, at):
    _, samples, width = mixed.shape
    mixed[at : at + rows.shape[0] // samples] = (
        dot(rows, w_mix[...]).astype(BF16).reshape(-1, samples, width)
    )


def project_kernel(own, partner, w_cell, w_mix, proj, mixed, own_in, sem):
    columns = own.shape[0]
    copy = pltpu.make_async_copy(own, own_in, sem)
    copy.start()
    rows = first_projection([partner[...]], w_cell, proj, columns)
    second_projection(rows, w_mix, mixed, columns)
    copy.wait()
    rows = first_projection([own_in[...]], w_cell, proj, 0)
    second_projection(rows, w_mix, mixed, 0)


def chip_kernel(score_scale, index, proj, mixed, w_pool, _, out, pool_in, pool_x, pool_y, sem):
    copy = pltpu.make_async_copy(w_pool, pool_in, sem)
    copy.start()
    out[...] = jnp.zeros(out.shape, F32)
    lists = [(index, 0)]
    attend_lists(lists, 0, proj, mixed, score_scale, pool_x, pool_y)
    copy.wait()
    score_lists(lists, pool_in, out, pool_x, pool_y)


def attend_pairs(pairs, proj, mixed, score_scale):
    samples = proj.shape[1]
    shape = (samples, 2 * samples)
    lane = lax.broadcasted_iota(jnp.int32, shape, 1)
    first = lane < samples
    unit = (lax.rem(lane, samples) == lax.broadcasted_iota(jnp.int32, shape, 0)).astype(F32)
    weights = []
    for x, y in pairs:
        both = dot_nt(
            jnp.concatenate([proj[y], proj[x]], axis=0), jnp.concatenate([proj[x], proj[y]], axis=0)
        )
        weights.append(jnp.where(first, both[:samples], both[samples:]) * score_scale)
    weights = [jnp.exp(w - jnp.max(w, axis=0, keepdims=True)) for w in weights]
    weights = [w * (1.0 / jnp.sum(w, axis=0, keepdims=True)) for w in weights]
    attend = [
        jnp.transpose(
            jnp.concatenate([jnp.where(first, w, unit), jnp.where(first, unit, w)], axis=0)
        ).astype(BF16)
        for w in weights
    ]
    pooled = []
    for t, (x, y) in zip(attend, pairs):
        rows = jnp.tanh(dot(t, jnp.concatenate([mixed[y], mixed[x]], axis=0)))
        pooled.append(
            [jnp.sum(r, axis=0, keepdims=True) * (1.0 / samples) for r in (rows[:samples], rows[samples:])]
        )
    return pooled


def lists_of(held, index):
    return [(ref, 8 * at) for ref, number in zip(index, held) for at in range(number)]


def near_kernel(chips, base, held, score_scale, *refs):
    count = len(held)
    lists, remote = refs[:count], refs[count : count + chips]
    w_cell, w_mix, _, _, proj, mixed, pool_x, pool_y = refs[count + chips : -1 - count]
    index, sems = refs[-1 - count : -1], refs[-1]
    copies = [
        pltpu.make_async_copy(ref, held_in, sems.at[i])
        for i, (ref, held_in) in enumerate(zip(lists, index))
    ]
    for copy in copies:
        copy.start()
    rows = first_projection([ref[...] for ref in remote], w_cell, proj, base)
    second_projection(rows, w_mix, mixed, base)
    for copy in copies:
        copy.wait()
    attend_lists(lists_of(held, index), 0, proj, mixed, score_scale, pool_x, pool_y)


def far_kernel(held, near, score_scale, *refs):
    count = len(held)
    index = refs[:count]
    proj, mixed, w_pool, before, _, _, out, pool_x, pool_y = refs[count:]
    lists = lists_of(held, index)
    attend_lists(lists, near, proj, mixed, score_scale, pool_x, pool_y)
    out[...] = before[...]
    score_lists(lists, w_pool, out, pool_x, pool_y)


def starts_of(lists):
    starts = [0]
    for ref, row in lists:
        starts.append(starts[-1] + ref[row + TOTAL, 0])
    return starts


def attend_lists(lists, done, proj, mixed, score_scale, pool_x, pool_y):
    lanes = lists[0][0].shape[1]
    starts = starts_of(lists)
    todo = list(zip(lists, starts))[done:]
    lane = lax.broadcasted_iota(jnp.int32, (1, LANES), 1)

    def column(at):
        found = [0, 0, 0, 0]
        for (ref, row), start in todo:
            here = jnp.clip(at - start, 0, lanes - 1)
            found = [
                jnp.where(at >= start, ref[row + field, here], value)
                for field, value in zip((IX, IY, READER, SLOT), found)
            ]
        return found

    def step(first, size, i, carry):
        at = [first + i * size + u for u in range(size)]
        columns = [column(p) for p in at]
        pooled = attend_pairs([(x, y) for x, y, _, _ in columns], proj, mixed, score_scale)
        for p, (_, _, reader, slot), (row_x, row_y) in zip(at, columns, pooled):
            tag = jnp.where(lane == 0, reader, slot).astype(F32)
            pool_x[pl.ds(p, 1)] = jnp.concatenate([row_x, tag], axis=1)
            pool_y[pl.ds(p, 1)] = row_y
        return carry

    large, middle, small = STEPS
    left = starts[-1] - starts[done]
    rest = lax.rem(left, large)
    counts = (
        left // large + (rest > middle + small).astype(jnp.int32),
        ((rest > small) & (rest <= middle + small)).astype(jnp.int32),
        (((rest > 0) & (rest <= small)) | ((rest > middle) & (rest <= middle + small))).astype(jnp.int32),
    )
    first = starts[done]
    for size, count in zip(STEPS, counts):
        lax.fori_loop(0, count, functools.partial(step, first, size), 0)
        first = first + size * count


def score_lists(lists, w_pool, out, pool_x, pool_y):
    total = starts_of(lists)[-1]
    block = LANES // 2
    width = w_pool.shape[0]
    readers, slots = out.shape

    def step(i, carry):
        here = pl.ds(pl.multiple_of(i * block, block), block)
        pooled = jnp.concatenate([pool_x[here, :width], pool_y[here]], axis=0).astype(BF16)
        z = dot(pooled, w_pool[...])
        zx, zy = z[:block], z[block:]
        inner = jnp.mean(zx * zy, axis=1, keepdims=True)
        norms = (jnp.mean(zx * zx, axis=1, keepdims=True) + EPSILON) * (
            jnp.mean(zy * zy, axis=1, keepdims=True) + EPSILON
        )
        score = inner / jnp.sqrt(norms) / SOFTMAX_WARMTH
        live = lax.broadcasted_iota(jnp.int32, (block, 1), 0) < total - i * block
        tags = jnp.where(live, pool_x[here, width:], -1.0).astype(jnp.int32)
        score = jnp.where(live, score, 0.0)
        of_reader = tags[:, :1] == lax.broadcasted_iota(jnp.int32, (block, readers), 1)
        of_slot = tags[:, 1:2] == lax.broadcasted_iota(jnp.int32, (block, slots), 1)
        out[...] += lax.dot_general(
            jnp.where(of_reader, score, 0.0),
            of_slot.astype(F32),
            (((0,), (0,)), ((), ())),
            preferred_element_type=F32,
            precision=lax.Precision.HIGHEST,
        )
        return carry

    lax.fori_loop(0, (total + block - 1) // block, step, 0)


def share_kernel(quarter, cells, share, sem):
    first = lax.axis_index("grp") * quarter
    copy = pltpu.make_async_copy(cells.at[pl.ds(first, quarter)], share, sem)
    copy.start()
    copy.wait()


def prepare_kernel(sizes, pairs, counts, w_cell, w_mix, _, ids, own_list, cell_in, mix_in, held, sems):
    lines, shards, per_shard, pair_dev = sizes
    line, shard = lax.axis_index("grp"), lax.axis_index("shard")
    copy_cell = pltpu.make_async_copy(w_cell, cell_in, sems.at[0])
    copy_pairs = pltpu.make_async_copy(pairs, held, sems.at[1])
    copy_mix = pltpu.make_async_copy(w_mix, mix_in, sems.at[2])
    copy_pairs.start()
    copy_cell.start()
    copy_mix.start()
    copy_pairs.wait()
    slot = lax.broadcasted_iota(jnp.int32, ids.shape, 1)
    a, b = held[:1], held[1:]
    live = slot < counts[0]
    ids[...] = jnp.where(live, a * (shards * per_shard) + b, -1)
    mine = live & (b // (2 * per_shard) == shard // 2)
    x = lax.rem(a, per_shard)
    y = lax.rem(b, per_shard) + per_shard * lax.rem(b // per_shard + shard, 2)
    reader = jnp.full_like(slot, line * shards + shard)
    own_list[...] = pack_list(mine, (x, y, reader, slot), own_list.shape[1])
    copy_cell.wait()
    copy_mix.wait()


def pack_list(mine, values, lanes):
    rows, slots = mine.shape
    earlier = (
        lax.broadcasted_iota(jnp.int32, (slots, slots), 0)
        < lax.broadcasted_iota(jnp.int32, (slots, slots), 1)
    ).astype(BF16)
    place = lax.broadcasted_iota(jnp.int32, (lanes, slots), 0)
    field = lax.broadcasted_iota(jnp.int32, (8, slots), 0)
    before = dot(mine.astype(BF16), earlier)
    row_total = jnp.sum(mine.astype(F32), axis=1, keepdims=True)
    total = jnp.zeros((1, 1), F32)
    packed = jnp.zeros((8, lanes), F32)
    for r in range(rows):
        position = (before[r : r + 1] + total).astype(jnp.int32)
        position = jnp.where(mine[r : r + 1], position, -1)
        total = total + row_total[r : r + 1]
        chosen = (place == position).astype(BF16)
        fields = jnp.where(field == VALID, 1, 0)
        for which, value in zip((IX, IY, READER, SLOT), values):
            fields = jnp.where(field == which, value[r : r + 1], fields)
        packed = packed + dot_nt(fields.astype(BF16), chosen)
    row = lax.broadcasted_iota(jnp.int32, (8, lanes), 0)
    return jnp.where(row == TOTAL, total, packed).astype(jnp.int32)


def route_kernel(sizes, whose, *refs):
    lines, shards, per_shard, pair_dev = sizes
    ids_refs, out_refs = refs[:lines], refs[lines + 1 :]
    total_columns = shards * per_shard
    chip_columns = 2 * per_shard
    chips = shards // 2
    quarter = per_shard // lines
    line = lax.axis_index("grp")
    shard = lax.axis_index("shard")
    chip, core = shard // 2, lax.rem(shard, 2)
    ids = jnp.concatenate([ref[...] for ref in ids_refs], axis=0)
    live = ids >= 0
    kept = jnp.maximum(ids, 0)
    a = kept // total_columns
    b = kept - a * total_columns
    b_chip = b // chip_columns
    b_shard = b // per_shard
    a_local = lax.rem(a, per_shard)
    b_local = lax.rem(b, per_shard)
    reader_row = lax.broadcasted_iota(jnp.int32, ids.shape, 0)
    reader_id = lax.rem(line + reader_row, lines) * shards + shard
    slot = lax.broadcasted_iota(jnp.int32, ids.shape, 1)
    b_own = b_local + per_shard * lax.rem(b_shard + core, 2)
    lanes = out_refs[0].shape[1]
    for group, out_ref in zip(whose, out_refs):
        for at, (kind, offset) in enumerate(group):
            base = chip_columns + (offset - 1) * quarter
            if kind in ("receive", "partner"):
                here = core if kind == "receive" else 1 - core
                source = ring_place(chip, chips, offset)
                mine = live & (b_shard == source * 2 + here) & (b_local // quarter == line)
                x = a_local if kind == "receive" else a_local + per_shard
                y = base + b_local - line * quarter
            else:
                target = ring_place(chip, chips, -offset)
                mine = live & (b_chip == target) & (a_local // quarter == line)
                x, y = b_own, base + a_local - line * quarter
            out_ref[8 * at : 8 * at + 8] = pack_list(mine, (x, y, reader_id, slot), lanes)


def ring_place(chip, chips, offset):
    half = chips // 2
    place = jnp.where(chip < half, 2 * chip, 2 * (chip - half) + 1)
    other = lax.rem(place + offset + 2 * chips, chips)
    return other // 2 + half * lax.rem(other, 2)


def ring_of(chips):
    half = chips // 2
    return [p // 2 + half * (p % 2) for p in range(chips)]


def local(mesh_shape, cells, w_cell, w_mix, w_pool, pairs, counts):
    lines, shards = mesh_shape["grp"], mesh_shape["shard"]
    chips = shards // 2
    per_shard, samples, width = cells.shape
    pair_dev = pairs.shape[0]
    quarter = per_shard // lines
    score_scale = 1.0 / math.sqrt(width)
    ring = ring_of(chips)

    def from_ahead(offset):
        return [
            (2 * ring[(p + offset) % chips] + c, 2 * ring[p] + c) for p in range(chips) for c in (0, 1)
        ]

    offsets = range(1, chips // 2 + 1)
    swap = [(s, s ^ 1) for s in range(shards)]
    sizes = (lines, shards, per_shard, pair_dev)
    most = lines * min(pair_dev, 4 * pair_dev // shards)
    lanes = -(-max(most, pair_dev) // LANES) * LANES
    weight = jax.ShapeDtypeStruct(w_cell.shape, BF16)
    weight_bytes = 2 * width * width
    share = pl.pallas_call(
        functools.partial(share_kernel, quarter),
        out_shape=jax.ShapeDtypeStruct((quarter, samples, width), BF16),
        in_specs=[hbm()],
        out_specs=vmem(),
        scratch_shapes=[pltpu.SemaphoreType.DMA(())],
        compiler_params=pltpu.CompilerParams(vmem_limit_bytes=4 * 2**20),
        name="share",
    )(in_hbm(cells))
    remote = {d: lax.ppermute(share, "shard", from_ahead(d)) for d in offsets}
    cells, _ = lax.optimization_barrier((cells, share))
    partner = lax.ppermute(cells, "shard", swap)
    ids, own_list, w_cell, w_mix = pl.pallas_call(
        functools.partial(prepare_kernel, sizes),
        out_shape=(
            jax.ShapeDtypeStruct((1, pair_dev), jnp.int32),
            jax.ShapeDtypeStruct((8, lanes), jnp.int32),
            weight,
            weight,
        ),
        in_specs=[hbm(), smem(), hbm(), hbm(), pl.BlockSpec(memory_space=pl.ANY)],
        out_specs=[vmem()] * 4,
        scratch_shapes=[pltpu.VMEM((2, pair_dev), jnp.int32), pltpu.SemaphoreType.DMA((3,))],
        compiler_params=pltpu.CompilerParams(vmem_limit_bytes=2 * weight_bytes + 4 * 2**20),
        name="prepare",
    )(in_hbm(pairs.T), counts, in_hbm(w_cell), in_hbm(w_mix), share)
    ids = [ids] + [
        lax.ppermute(ids, "grp", [((g + k) % lines, g) for g in range(lines)])
        for k in range(1, lines)
    ]

    store = jax.ShapeDtypeStruct((2 * per_shard + len(offsets) * quarter, samples, width), BF16)
    scores = jax.ShapeDtypeStruct((lines * shards, pair_dev), F32)
    store_bytes = 2 * math.prod(store.shape)
    weight_bytes = 2 * width * width

    def pools(count):
        rows = count * lanes + LANES
        return [jax.ShapeDtypeStruct((rows, n), F32) for n in (width + LANES, width)]

    def limit(spare):
        return pltpu.CompilerParams(
            vmem_limit_bytes=2 * store_bytes + 3 * weight_bytes + spare * 2**20
        )

    proj, mixed = pl.pallas_call(
        project_kernel,
        out_shape=[store, store],
        in_specs=[hbm()] + [vmem()] * 3,
        out_specs=[vmem()] * 2,
        scratch_shapes=[pltpu.VMEM(cells.shape, BF16), pltpu.SemaphoreType.DMA(())],
        compiler_params=limit(16),
        name="project",
    )(in_hbm(cells), partner, w_cell, w_mix)

    groups = [offsets[i : i + 2] for i in range(0, len(offsets), 2)]
    whose, spans = [], []
    for group in groups:
        near = [[(kind, d) for d in group] for kind in ("receive", "partner")]
        far = [[("send", d)] for d in group if 2 * d != chips]
        spans.append((len(whose), len(whose) + len(near), len(whose) + len(near + far)))
        whose += near + far
    lists = pl.pallas_call(
        functools.partial(route_kernel, sizes, whose),
        out_shape=[jax.ShapeDtypeStruct((8 * len(kinds), lanes), jnp.int32) for kinds in whose],
        in_specs=[vmem()] * lines + [pl.BlockSpec(memory_space=pl.ANY)],
        out_specs=[vmem()] * len(whose),
        compiler_params=pltpu.CompilerParams(vmem_limit_bytes=4 * 2**20),
        name="route",
    )(*ids, proj)
    arrived = []
    for kinds, packed in zip(whose, lists):
        kind, d = kinds[0]
        if kind == "partner":
            packed = lax.ppermute(packed, "shard", swap)
        elif kind == "send":
            packed = lax.ppermute(packed, "shard", from_ahead(d))
        arrived.append(packed)

    out, w_pool = pl.pallas_call(
        functools.partial(chip_kernel, score_scale),
        out_shape=[scores, weight],
        in_specs=[smem(), vmem(), vmem(), hbm(), pl.BlockSpec(memory_space=pl.ANY)],
        out_specs=[vmem()] * 2,
        scratch_shapes=[
            *(pltpu.VMEM(x.shape, F32) for x in pools(1)),
            pltpu.SemaphoreType.DMA(()),
        ],
        compiler_params=limit(16),
        name="chip",
    )(own_list, proj, mixed, in_hbm(w_pool), lists[-1])

    for group, (first, middle, last) in zip(groups, spans):
        use = arrived[first:last]
        held = [x.shape[0] // 8 for x in use]
        number = middle - first
        at = number + len(group) + 2
        proj, mixed, *pooled = pl.pallas_call(
            functools.partial(
                near_kernel,
                len(group),
                2 * per_shard + (group[0] - 1) * quarter,
                held[:number],
                score_scale,
            ),
            out_shape=[store, store, *pools(sum(held))],
            in_specs=[vmem()] * (number + len(group) + 4),
            out_specs=[vmem()] * 4,
            input_output_aliases={at: 0, at + 1: 1},
            scratch_shapes=[
                *(pltpu.SMEM(x.shape, jnp.int32) for x in use[:number]),
                pltpu.SemaphoreType.DMA((number,)),
            ],
            compiler_params=limit(20),
            name="near" + "_".join(map(str, group)),
        )(*use[:number], *(remote[d] for d in group), w_cell, w_mix, proj, mixed)
        at = len(use) + 3
        out, *_ = pl.pallas_call(
            functools.partial(far_kernel, held, sum(held[:number]), score_scale),
            out_shape=[scores, *pools(sum(held))],
            in_specs=[smem()] * len(use) + [vmem()] * 6,
            out_specs=[vmem()] * 3,
            input_output_aliases={at: 0, at + 1: 1, at + 2: 2},
            compiler_params=limit(20),
            name="far" + "_".join(map(str, group)),
        )(*use, proj, mixed, w_pool, out, *pooled)

    back = lax.all_to_all(out, ("grp", "shard"), 0, 0, tiled=True)
    return jnp.sum(back, axis=0)


def solution(mesh):
    placed = (P("shard", None, None), P(), P(), P(), P(("grp", "shard"), None), P(("grp", "shard")))
    return jax.shard_map(
        functools.partial(local, dict(mesh.shape)),
        mesh=mesh,
        in_specs=placed,
        out_specs=P(("grp", "shard")),
        check_vma=False,
    )
```

```python
import functools
import math

import jax
import jax.numpy as jnp
from jax import lax
from jax.experimental import pallas as pl
from jax.experimental.pallas import tpu as pltpu
from jax.sharding import PartitionSpec as P

SOFTMAX_WARMTH = 0.07
EPSILON = 1e-06
LANES = 128
STEPS = (16, 8, 4)
F32 = jnp.float32
BF16 = jnp.bfloat16
NT = (((1,), (1,)), ((), ()))
CODE_BITS = 8


def vmem():
    return pl.BlockSpec(memory_space=pltpu.VMEM)


def hbm():
    return pl.BlockSpec(memory_space=pltpu.HBM)


def in_hbm(x):
    return pltpu.with_memory_space_constraint(x, pltpu.HBM)


def smem():
    return pl.BlockSpec(memory_space=pltpu.SMEM)


def dot(a, b):
    return jnp.dot(a, b, preferred_element_type=F32)


def dot_nt(a, b):
    return lax.dot_general(a, b, NT, preferred_element_type=F32)


def first_projection(blocks, w_cell, proj, at):
    _, samples, width = blocks[0].shape
    cells = jnp.concatenate([block.reshape(-1, width) for block in blocks], axis=0)
    rows = dot(cells, w_cell[...]).astype(BF16)
    proj[at : at + rows.shape[0] // samples] = rows.reshape(-1, samples, width)
    return rows


def second_projection(rows, w_mix, mixed, at):
    _, samples, width = mixed.shape
    mixed[at : at + rows.shape[0] // samples] = (
        dot(rows, w_mix[...]).astype(BF16).reshape(-1, samples, width)
    )


def project_kernel(own, partner, w_cell, w_mix, proj, mixed, own_in, sem):
    columns = own.shape[0]
    copy = pltpu.make_async_copy(own, own_in, sem)
    copy.start()
    rows = first_projection([partner[...]], w_cell, proj, columns)
    second_projection(rows, w_mix, mixed, columns)
    copy.wait()
    rows = first_projection([own_in[...]], w_cell, proj, 0)
    second_projection(rows, w_mix, mixed, 0)


def chip_kernel(score_scale, index, proj, mixed, w_pool, _, out, pool_in, pool_x, pool_y, sem):
    copy = pltpu.make_async_copy(w_pool, pool_in, sem)
    copy.start()
    out[...] = jnp.zeros(out.shape, F32)
    lists = [(index, 0)]
    attend_lists(lists, 0, proj, mixed, score_scale, pool_x, pool_y)
    copy.wait()
    score_lists(lists, pool_in, out, pool_x, pool_y)


def attend_pairs(pairs, proj, mixed, score_scale):
    samples = proj.shape[1]
    shape = (samples, 2 * samples)
    lane = lax.broadcasted_iota(jnp.int32, shape, 1)
    first = lane < samples
    unit = (lax.rem(lane, samples) == lax.broadcasted_iota(jnp.int32, shape, 0)).astype(F32)
    weights = []
    for x, y in pairs:
        both = dot_nt(
            jnp.concatenate([proj[y], proj[x]], axis=0), jnp.concatenate([proj[x], proj[y]], axis=0)
        )
        weights.append(jnp.where(first, both[:samples], both[samples:]) * score_scale)
    weights = [jnp.exp(w - jnp.max(w, axis=0, keepdims=True)) for w in weights]
    weights = [w * (1.0 / jnp.sum(w, axis=0, keepdims=True)) for w in weights]
    attend = [
        jnp.transpose(
            jnp.concatenate([jnp.where(first, w, unit), jnp.where(first, unit, w)], axis=0)
        ).astype(BF16)
        for w in weights
    ]
    pooled = []
    for t, (x, y) in zip(attend, pairs):
        rows = jnp.tanh(dot(t, jnp.concatenate([mixed[y], mixed[x]], axis=0)))
        pooled.append(
            [jnp.sum(r, axis=0, keepdims=True) * (1.0 / samples) for r in (rows[:samples], rows[samples:])]
        )
    return pooled


def lists_of(held, index):
    return [(ref, 2 * at) for ref, number in zip(index, held) for at in range(number)]


def start_copies(sources, targets, sems):
    copies = [
        pltpu.make_async_copy(source, target, sems.at[i])
        for i, (source, target) in enumerate(zip(sources, targets))
    ]
    for copy in copies:
        copy.start()
    return copies


def near_kernel(chips, base, held, score_scale, *refs):
    count = len(held)
    lists, remote = refs[:count], refs[count : count + chips]
    w_cell, w_mix, _, _, proj, mixed, pool_x, pool_y = refs[count + chips : -1 - count]
    index, sems = refs[-1 - count : -1], refs[-1]
    copies = start_copies(lists, index, sems)
    rows = first_projection([ref[...] for ref in remote], w_cell, proj, base)
    second_projection(rows, w_mix, mixed, base)
    for copy in copies:
        copy.wait()
    attend_lists(lists_of(held, index), 0, proj, mixed, score_scale, pool_x, pool_y, last=False)


def far_kernel(held, near, score_scale, *refs):
    count = len(held)
    lists = refs[:count]
    proj, mixed, w_pool, before, _, _, out, pool_x, pool_y = refs[count : -1 - count]
    index, sems = refs[-1 - count : -1], refs[-1]
    copies = start_copies(lists, index, sems)
    out[...] = before[...]
    for copy in copies:
        copy.wait()
    every = lists_of(held, index)
    attend_lists(every, near, proj, mixed, score_scale, pool_x, pool_y)
    score_lists(every, w_pool, out, pool_x, pool_y)


def starts_of(lists):
    starts = [0]
    for ref, row in lists:
        starts.append(starts[-1] + ref[row + 1, 0])
    return starts


def attend_lists(lists, near, proj, mixed, score_scale, pool_x, pool_y, last=True):
    lanes = lists[0][0].shape[1]
    starts = starts_of(lists)
    todo = list(zip(lists, starts))
    lane = lax.broadcasted_iota(jnp.int32, (1, LANES), 1)

    def column(at):
        code = 0
        for (ref, row), start in todo:
            here = jnp.clip(at - start, 0, lanes - 1)
            code = jnp.where(at >= start, ref[row, here], code)
        mask = 2**CODE_BITS - 1
        return (
            code & mask,
            (code >> CODE_BITS) & mask,
            (code >> 2 * CODE_BITS) & mask,
            code >> 3 * CODE_BITS,
        )

    def step(first, size, i, carry):
        at = [first + i * size + u for u in range(size)]
        columns = [column(p) for p in at]
        pooled = attend_pairs([(x, y) for x, y, _, _ in columns], proj, mixed, score_scale)
        for p, (_, _, reader, slot), (row_x, row_y) in zip(at, columns, pooled):
            tag = jnp.where(lane == 0, reader, slot).astype(F32)
            pool_x[pl.ds(p, 1)] = jnp.concatenate([row_x, tag], axis=1)
            pool_y[pl.ds(p, 1)] = row_y
        return carry

    large, middle, small = STEPS
    first = starts[near] // large * large
    left = starts[-1] - first
    rest = lax.rem(left, large) if last else jnp.int32(0)
    counts = (
        left // large + (rest > middle + small).astype(jnp.int32),
        ((rest > small) & (rest <= middle + small)).astype(jnp.int32),
        (((rest > 0) & (rest <= small)) | ((rest > middle) & (rest <= middle + small))).astype(jnp.int32),
    )
    for size, count in zip(STEPS if last else STEPS[:1], counts):
        lax.fori_loop(0, count, functools.partial(step, first, size), 0)
        first = first + size * count


def score_lists(lists, w_pool, out, pool_x, pool_y):
    total = starts_of(lists)[-1]
    block = LANES // 2
    width = w_pool.shape[0]
    readers, slots = out.shape

    def step(i, carry):
        here = pl.ds(pl.multiple_of(i * block, block), block)
        pooled = jnp.concatenate([pool_x[here, :width], pool_y[here]], axis=0).astype(BF16)
        z = dot(pooled, w_pool[...])
        zx, zy = z[:block], z[block:]
        inner = jnp.mean(zx * zy, axis=1, keepdims=True)
        norms = (jnp.mean(zx * zx, axis=1, keepdims=True) + EPSILON) * (
            jnp.mean(zy * zy, axis=1, keepdims=True) + EPSILON
        )
        score = inner / jnp.sqrt(norms) / SOFTMAX_WARMTH
        live = lax.broadcasted_iota(jnp.int32, (block, 1), 0) < total - i * block
        tags = jnp.where(live, pool_x[here, width:], -1.0).astype(jnp.int32)
        score = jnp.where(live, score, 0.0)
        of_reader = tags[:, :1] == lax.broadcasted_iota(jnp.int32, (block, readers), 1)
        of_slot = tags[:, 1:2] == lax.broadcasted_iota(jnp.int32, (block, slots), 1)
        out[...] += lax.dot_general(
            jnp.where(of_reader, score, 0.0),
            of_slot.astype(F32),
            (((0,), (0,)), ((), ())),
            preferred_element_type=F32,
            precision=lax.Precision.HIGHEST,
        )
        return carry

    lax.fori_loop(0, (total + block - 1) // block, step, 0)


def share_kernel(quarter, cells, share, sem):
    first = lax.axis_index("grp") * quarter
    copy = pltpu.make_async_copy(cells.at[pl.ds(first, quarter)], share, sem)
    copy.start()
    copy.wait()


def prepare_kernel(sizes, pairs, counts, w_cell, w_mix, _, ids, own_list, cell_in, mix_in, held, sems):
    lines, shards, per_shard, pair_dev = sizes
    line, shard = lax.axis_index("grp"), lax.axis_index("shard")
    copy_cell = pltpu.make_async_copy(w_cell, cell_in, sems.at[0])
    copy_pairs = pltpu.make_async_copy(pairs, held, sems.at[1])
    copy_mix = pltpu.make_async_copy(w_mix, mix_in, sems.at[2])
    copy_pairs.start()
    copy_cell.start()
    copy_mix.start()
    copy_pairs.wait()
    slot = lax.broadcasted_iota(jnp.int32, ids.shape, 1)
    a, b = held[:1], held[1:]
    live = slot < counts[0]
    ids[...] = jnp.where(live, a * (shards * per_shard) + b, -1)
    mine = live & (b // (2 * per_shard) == shard // 2)
    x = lax.rem(a, per_shard)
    y = lax.rem(b, per_shard) + per_shard * lax.rem(b // per_shard + shard, 2)
    reader = jnp.full_like(slot, line * shards + shard)
    own_list[...] = pack_list(mine, (x, y, reader, slot), own_list.shape[1])
    copy_cell.wait()
    copy_mix.wait()


def pack_list(mine, values, lanes):
    rows, slots = mine.shape
    earlier = (
        lax.broadcasted_iota(jnp.int32, (slots, slots), 0)
        < lax.broadcasted_iota(jnp.int32, (slots, slots), 1)
    ).astype(BF16)
    place = lax.broadcasted_iota(jnp.int32, (lanes, slots), 0)
    field = lax.broadcasted_iota(jnp.int32, (8, slots), 0)
    before = dot(mine.astype(BF16), earlier)
    row_total = jnp.sum(mine.astype(F32), axis=1, keepdims=True)
    total = jnp.zeros((1, 1), F32)
    packed = jnp.zeros((8, lanes), F32)
    for r in range(rows):
        position = (before[r : r + 1] + total).astype(jnp.int32)
        position = jnp.where(mine[r : r + 1], position, -1)
        total = total + row_total[r : r + 1]
        chosen = (place == position).astype(BF16)
        fields = jnp.zeros_like(field)
        for which, value in enumerate(values):
            fields = jnp.where(field == which, value[r : r + 1], fields)
        packed = packed + dot_nt(fields.astype(BF16), chosen)
    packed = packed.astype(jnp.int32)
    code = packed[:1]
    for which in range(1, len(values)):
        code = code + packed[which : which + 1] * 2 ** (which * CODE_BITS)
    return jnp.concatenate([code, jnp.broadcast_to(total, code.shape).astype(jnp.int32)], axis=0)


def route_kernel(sizes, whose, *refs):
    lines, shards, per_shard, pair_dev = sizes
    ids_refs, out_refs = refs[:lines], refs[lines + 1 :]
    total_columns = shards * per_shard
    chip_columns = 2 * per_shard
    chips = shards // 2
    quarter = per_shard // lines
    line = lax.axis_index("grp")
    shard = lax.axis_index("shard")
    chip, core = shard // 2, lax.rem(shard, 2)
    ids = jnp.concatenate([ref[...] for ref in ids_refs], axis=0)
    live = ids >= 0
    kept = jnp.maximum(ids, 0)
    a = kept // total_columns
    b = kept - a * total_columns
    b_chip = b // chip_columns
    b_shard = b // per_shard
    a_local = lax.rem(a, per_shard)
    b_local = lax.rem(b, per_shard)
    reader_row = lax.broadcasted_iota(jnp.int32, ids.shape, 0)
    reader_id = lax.rem(line + reader_row, lines) * shards + shard
    slot = lax.broadcasted_iota(jnp.int32, ids.shape, 1)
    b_own = b_local + per_shard * lax.rem(b_shard + core, 2)
    lanes = out_refs[0].shape[1]
    for group, out_ref in zip(whose, out_refs):
        for at, (kind, offset) in enumerate(group):
            base = chip_columns + (offset - 1) * quarter
            if kind in ("receive", "partner"):
                here = core if kind == "receive" else 1 - core
                source = ring_place(chip, chips, offset)
                mine = live & (b_shard == source * 2 + here) & (b_local // quarter == line)
                x = a_local if kind == "receive" else a_local + per_shard
                y = base + b_local - line * quarter
            else:
                target = ring_place(chip, chips, -offset)
                mine = live & (b_chip == target) & (a_local // quarter == line)
                x, y = b_own, base + a_local - line * quarter
            out_ref[2 * at : 2 * at + 2] = pack_list(mine, (x, y, reader_id, slot), lanes)


def ring_place(chip, chips, offset):
    half = chips // 2
    place = jnp.where(chip < half, 2 * chip, 2 * (chip - half) + 1)
    other = lax.rem(place + offset + 2 * chips, chips)
    return other // 2 + half * lax.rem(other, 2)


def ring_of(chips):
    half = chips // 2
    return [p // 2 + half * (p % 2) for p in range(chips)]


def local(mesh_shape, cells, w_cell, w_mix, w_pool, pairs, counts):
    lines, shards = mesh_shape["grp"], mesh_shape["shard"]
    chips = shards // 2
    per_shard, samples, width = cells.shape
    pair_dev = pairs.shape[0]
    quarter = per_shard // lines
    score_scale = 1.0 / math.sqrt(width)
    ring = ring_of(chips)

    def from_ahead(offset):
        return [
            (2 * ring[(p + offset) % chips] + c, 2 * ring[p] + c) for p in range(chips) for c in (0, 1)
        ]

    offsets = range(1, chips // 2 + 1)
    swap = [(s, s ^ 1) for s in range(shards)]
    sizes = (lines, shards, per_shard, pair_dev)
    assert max(2 * per_shard + len(offsets) * quarter, lines * shards) <= 2**CODE_BITS
    assert pair_dev <= 2 ** (31 - 3 * CODE_BITS)
    most = lines * min(pair_dev, 4 * pair_dev // shards)
    lanes = -(-max(most, pair_dev) // LANES) * LANES
    weight = jax.ShapeDtypeStruct(w_cell.shape, BF16)
    weight_bytes = 2 * width * width
    share = pl.pallas_call(
        functools.partial(share_kernel, quarter),
        out_shape=jax.ShapeDtypeStruct((quarter, samples, width), BF16),
        in_specs=[hbm()],
        out_specs=vmem(),
        scratch_shapes=[pltpu.SemaphoreType.DMA(())],
        compiler_params=pltpu.CompilerParams(vmem_limit_bytes=4 * 2**20),
        name="share",
    )(in_hbm(cells))
    remote = {d: lax.ppermute(share, "shard", from_ahead(d)) for d in offsets}
    cells, _ = lax.optimization_barrier((cells, share))
    partner = lax.ppermute(cells, "shard", swap)
    ids, own_list, w_cell, w_mix = pl.pallas_call(
        functools.partial(prepare_kernel, sizes),
        out_shape=(
            jax.ShapeDtypeStruct((1, pair_dev), jnp.int32),
            jax.ShapeDtypeStruct((2, lanes), jnp.int32),
            weight,
            weight,
        ),
        in_specs=[hbm(), smem(), hbm(), hbm(), pl.BlockSpec(memory_space=pl.ANY)],
        out_specs=[vmem()] * 4,
        scratch_shapes=[pltpu.VMEM((2, pair_dev), jnp.int32), pltpu.SemaphoreType.DMA((3,))],
        compiler_params=pltpu.CompilerParams(vmem_limit_bytes=2 * weight_bytes + 4 * 2**20),
        name="prepare",
    )(in_hbm(pairs.T), counts, in_hbm(w_cell), in_hbm(w_mix), share)
    ids = [ids] + [
        lax.ppermute(ids, "grp", [((g + k) % lines, g) for g in range(lines)])
        for k in range(1, lines)
    ]

    store = jax.ShapeDtypeStruct((2 * per_shard + len(offsets) * quarter, samples, width), BF16)
    scores = jax.ShapeDtypeStruct((lines * shards, pair_dev), F32)
    store_bytes = 2 * math.prod(store.shape)
    weight_bytes = 2 * width * width

    def pools(count):
        rows = count * lanes + LANES
        return [jax.ShapeDtypeStruct((rows, n), F32) for n in (width + LANES, width)]

    def limit(spare):
        return pltpu.CompilerParams(
            vmem_limit_bytes=2 * store_bytes + 3 * weight_bytes + spare * 2**20
        )

    proj, mixed = pl.pallas_call(
        project_kernel,
        out_shape=[store, store],
        in_specs=[hbm()] + [vmem()] * 3,
        out_specs=[vmem()] * 2,
        scratch_shapes=[pltpu.VMEM(cells.shape, BF16), pltpu.SemaphoreType.DMA(())],
        compiler_params=limit(16),
        name="project",
    )(in_hbm(cells), partner, w_cell, w_mix)

    groups = [offsets[i : i + 2] for i in range(0, len(offsets), 2)]
    whose, spans = [], []
    for group in groups:
        near = [[(kind, d) for d in group] for kind in ("receive", "partner")]
        far = [[("send", d)] for d in group if 2 * d != chips]
        spans.append((len(whose), len(whose) + len(near), len(whose) + len(near + far)))
        whose += near + far
    lists = pl.pallas_call(
        functools.partial(route_kernel, sizes, whose),
        out_shape=[jax.ShapeDtypeStruct((2 * len(kinds), lanes), jnp.int32) for kinds in whose],
        in_specs=[vmem()] * lines + [pl.BlockSpec(memory_space=pl.ANY)],
        out_specs=[vmem()] * len(whose),
        compiler_params=pltpu.CompilerParams(vmem_limit_bytes=4 * 2**20),
        name="route",
    )(*ids, proj)
    arrived = []
    for kinds, packed in zip(whose, lists):
        kind, d = kinds[0]
        if kind == "partner":
            packed = lax.ppermute(packed, "shard", swap)
        elif kind == "send":
            packed = lax.ppermute(packed, "shard", from_ahead(d))
        arrived.append(packed)

    out, w_pool = pl.pallas_call(
        functools.partial(chip_kernel, score_scale),
        out_shape=[scores, weight],
        in_specs=[smem(), vmem(), vmem(), hbm(), pl.BlockSpec(memory_space=pl.ANY)],
        out_specs=[vmem()] * 2,
        scratch_shapes=[
            *(pltpu.VMEM(x.shape, F32) for x in pools(1)),
            pltpu.SemaphoreType.DMA(()),
        ],
        compiler_params=limit(16),
        name="chip",
    )(own_list, proj, mixed, in_hbm(w_pool), lists[-1])

    for group, (first, middle, last) in zip(groups, spans):
        use = arrived[first:last]
        held = [x.shape[0] // 2 for x in use]
        number = middle - first
        at = number + len(group) + 2
        proj, mixed, *pooled = pl.pallas_call(
            functools.partial(
                near_kernel,
                len(group),
                2 * per_shard + (group[0] - 1) * quarter,
                held[:number],
                score_scale,
            ),
            out_shape=[store, store, *pools(sum(held))],
            in_specs=[vmem()] * (number + len(group) + 4),
            out_specs=[vmem()] * 4,
            input_output_aliases={at: 0, at + 1: 1},
            scratch_shapes=[
                *(pltpu.SMEM(x.shape, jnp.int32) for x in use[:number]),
                pltpu.SemaphoreType.DMA((number,)),
            ],
            compiler_params=limit(20),
            name="near" + "_".join(map(str, group)),
        )(*use[:number], *(remote[d] for d in group), w_cell, w_mix, proj, mixed)
        at = len(use) + 3
        out, *_ = pl.pallas_call(
            functools.partial(far_kernel, held, sum(held[:number]), score_scale),
            out_shape=[scores, *pools(sum(held))],
            in_specs=[vmem()] * (len(use) + 6),
            out_specs=[vmem()] * 3,
            input_output_aliases={at: 0, at + 1: 1, at + 2: 2},
            scratch_shapes=[
                *(pltpu.SMEM(x.shape, jnp.int32) for x in use),
                pltpu.SemaphoreType.DMA((len(use),)),
            ],
            compiler_params=limit(20),
            name="far" + "_".join(map(str, group)),
        )(*use, proj, mixed, w_pool, out, *pooled)

    back = lax.all_to_all(out, ("grp", "shard"), 0, 0, tiled=True)
    return jnp.sum(back, axis=0)


def solution(mesh):
    placed = (P("shard", None, None), P(), P(), P(), P(("grp", "shard"), None), P(("grp", "shard")))
    return jax.shard_map(
        functools.partial(local, dict(mesh.shape)),
        mesh=mesh,
        in_specs=placed,
        out_specs=P(("grp", "shard")),
        check_vma=False,
    )
```

```python
import functools
import math

import jax
import jax.numpy as jnp
from jax import lax
from jax.experimental import pallas as pl
from jax.experimental.pallas import tpu as pltpu
from jax.sharding import PartitionSpec as P

SOFTMAX_WARMTH = 0.07
EPSILON = 1e-06
LANES = 128
STEPS = (16, 8, 4)
F32 = jnp.float32
BF16 = jnp.bfloat16
NT = (((1,), (1,)), ((), ()))
CODE_BITS = 8


def vmem():
    return pl.BlockSpec(memory_space=pltpu.VMEM)


def hbm():
    return pl.BlockSpec(memory_space=pltpu.HBM)


def in_hbm(x):
    return pltpu.with_memory_space_constraint(x, pltpu.HBM)


def smem():
    return pl.BlockSpec(memory_space=pltpu.SMEM)


def dot(a, b):
    return jnp.dot(a, b, preferred_element_type=F32)


def dot_nt(a, b):
    return lax.dot_general(a, b, NT, preferred_element_type=F32)


def first_projection(block, w_cell, proj, at):
    columns, samples, width = block.shape
    rows = dot(block.reshape(-1, width), w_cell[...]).astype(BF16)
    proj[at : at + columns] = rows.reshape(columns, samples, width)
    return rows


def second_projection(rows, w_mix, mixed, at):
    _, samples, width = mixed.shape
    mixed[at : at + rows.shape[0] // samples] = (
        dot(rows, w_mix[...]).astype(BF16).reshape(-1, samples, width)
    )


def project_kernel(own, partner, w_cell, w_mix, proj, mixed, own_in, sem):
    columns = own.shape[0]
    copy = pltpu.make_async_copy(own, own_in, sem)
    copy.start()
    rows = first_projection(partner[...], w_cell, proj, columns)
    second_projection(rows, w_mix, mixed, columns)
    copy.wait()
    rows = first_projection(own_in[...], w_cell, proj, 0)
    second_projection(rows, w_mix, mixed, 0)


def chip_kernel(score_scale, index, proj, mixed, w_pool, _, out, pool_in, pool_x, pool_y, sem):
    copy = pltpu.make_async_copy(w_pool, pool_in, sem)
    copy.start()
    out[...] = jnp.zeros(out.shape, F32)
    lists = [(index, 0)]
    attend_lists(lists, 0, proj, mixed, score_scale, pool_x, pool_y)
    copy.wait()
    score_lists(lists, pool_in, out, pool_x, pool_y)


def attend_pairs(pairs, proj, mixed, score_scale):
    samples = proj.shape[1]
    shape = (samples, 2 * samples)
    lane = lax.broadcasted_iota(jnp.int32, shape, 1)
    first = lane < samples
    unit = (lax.rem(lane, samples) == lax.broadcasted_iota(jnp.int32, shape, 0)).astype(F32)
    weights = []
    for x, y in pairs:
        both = dot_nt(
            jnp.concatenate([proj[y], proj[x]], axis=0), jnp.concatenate([proj[x], proj[y]], axis=0)
        )
        weights.append(jnp.where(first, both[:samples], both[samples:]) * score_scale)
    weights = [jnp.exp(w - jnp.max(w, axis=0, keepdims=True)) for w in weights]
    weights = [w * (1.0 / jnp.sum(w, axis=0, keepdims=True)) for w in weights]
    attend = [
        jnp.transpose(
            jnp.concatenate([jnp.where(first, w, unit), jnp.where(first, unit, w)], axis=0)
        ).astype(BF16)
        for w in weights
    ]
    pooled = []
    for t, (x, y) in zip(attend, pairs):
        rows = jnp.tanh(dot(t, jnp.concatenate([mixed[y], mixed[x]], axis=0)))
        pooled.append(
            [jnp.sum(r, axis=0, keepdims=True) * (1.0 / samples) for r in (rows[:samples], rows[samples:])]
        )
    return pooled


def lists_of(held, index):
    return [(ref, 2 * at) for ref, number in zip(index, held) for at in range(number)]


def start_copies(sources, targets, sems):
    copies = [
        pltpu.make_async_copy(source, target, sems.at[i])
        for i, (source, target) in enumerate(zip(sources, targets))
    ]
    for copy in copies:
        copy.start()
    return copies


def near_kernel(chips, base, held, score_scale, *refs):
    count = len(held)
    lists, remote = refs[:count], refs[count : count + chips]
    w_cell, w_mix, _, _, proj, mixed, pool_x, pool_y = refs[count + chips : -1 - count]
    index, sems = refs[-1 - count : -1], refs[-1]
    copies = start_copies(lists, index, sems)
    places = [base + i * remote[0].shape[0] for i in range(chips)]
    rows = [first_projection(ref[...], w_cell, proj, at) for ref, at in zip(remote, places)]
    for block, at in zip(rows, places):
        second_projection(block, w_mix, mixed, at)
    for copy in copies:
        copy.wait()
    attend_lists(lists_of(held, index), 0, proj, mixed, score_scale, pool_x, pool_y, last=False)


def far_kernel(held, near, score_scale, *refs):
    count = len(held)
    lists = refs[:count]
    proj, mixed, w_pool, before, _, _, out, pool_x, pool_y = refs[count : -1 - count]
    index, sems = refs[-1 - count : -1], refs[-1]
    copies = start_copies(lists, index, sems)
    out[...] = before[...]
    for copy in copies:
        copy.wait()
    every = lists_of(held, index)
    attend_lists(every, near, proj, mixed, score_scale, pool_x, pool_y)
    score_lists(every, w_pool, out, pool_x, pool_y)


def starts_of(lists):
    starts = [0]
    for ref, row in lists:
        starts.append(starts[-1] + ref[row + 1, 0])
    return starts


def attend_lists(lists, near, proj, mixed, score_scale, pool_x, pool_y, last=True):
    lanes = lists[0][0].shape[1]
    starts = starts_of(lists)
    todo = list(zip(lists, starts))
    lane = lax.broadcasted_iota(jnp.int32, (1, LANES), 1)

    def column(at):
        code = 0
        for (ref, row), start in todo:
            here = jnp.clip(at - start, 0, lanes - 1)
            code = jnp.where(at >= start, ref[row, here], code)
        mask = 2**CODE_BITS - 1
        return (
            code & mask,
            (code >> CODE_BITS) & mask,
            (code >> 2 * CODE_BITS) & mask,
            code >> 3 * CODE_BITS,
        )

    def step(first, size, i, carry):
        at = [first + i * size + u for u in range(size)]
        columns = [column(p) for p in at]
        pooled = attend_pairs([(x, y) for x, y, _, _ in columns], proj, mixed, score_scale)
        for p, (_, _, reader, slot), (row_x, row_y) in zip(at, columns, pooled):
            tag = jnp.where(lane == 0, reader, slot).astype(F32)
            pool_x[pl.ds(p, 1)] = jnp.concatenate([row_x, tag], axis=1)
            pool_y[pl.ds(p, 1)] = row_y
        return carry

    large, middle, small = STEPS
    first = starts[near] // large * large
    left = starts[-1] - first
    rest = lax.rem(left, large) if last else jnp.int32(0)
    counts = (
        left // large + (rest > middle + small).astype(jnp.int32),
        ((rest > small) & (rest <= middle + small)).astype(jnp.int32),
        (((rest > 0) & (rest <= small)) | ((rest > middle) & (rest <= middle + small))).astype(jnp.int32),
    )
    for size, count in zip(STEPS if last else STEPS[:1], counts):
        lax.fori_loop(0, count, functools.partial(step, first, size), 0)
        first = first + size * count


def score_lists(lists, w_pool, out, pool_x, pool_y):
    total = starts_of(lists)[-1]
    block = LANES // 2
    width = w_pool.shape[0]
    readers, slots = out.shape

    def step(i, carry):
        here = pl.ds(pl.multiple_of(i * block, block), block)
        pooled = jnp.concatenate([pool_x[here, :width], pool_y[here]], axis=0).astype(BF16)
        z = dot(pooled, w_pool[...])
        zx, zy = z[:block], z[block:]
        inner = jnp.mean(zx * zy, axis=1, keepdims=True)
        norms = (jnp.mean(zx * zx, axis=1, keepdims=True) + EPSILON) * (
            jnp.mean(zy * zy, axis=1, keepdims=True) + EPSILON
        )
        score = inner / jnp.sqrt(norms) / SOFTMAX_WARMTH
        live = lax.broadcasted_iota(jnp.int32, (block, 1), 0) < total - i * block
        tags = jnp.where(live, pool_x[here, width:], -1.0).astype(jnp.int32)
        score = jnp.where(live, score, 0.0)
        of_reader = tags[:, :1] == lax.broadcasted_iota(jnp.int32, (block, readers), 1)
        of_slot = tags[:, 1:2] == lax.broadcasted_iota(jnp.int32, (block, slots), 1)
        out[...] += lax.dot_general(
            jnp.where(of_reader, score, 0.0),
            of_slot.astype(F32),
            (((0,), (0,)), ((), ())),
            preferred_element_type=F32,
            precision=lax.Precision.HIGHEST,
        )
        return carry

    lax.fori_loop(0, (total + block - 1) // block, step, 0)


def share_kernel(cells, share, sem):
    quarter = share.shape[0]
    first = lax.axis_index("grp") * quarter
    copy = pltpu.make_async_copy(cells.at[pl.ds(first, quarter)], share, sem)
    copy.start()
    copy.wait()


def prepare_kernel(sizes, pairs, counts, w_cell, w_mix, _, ids, own_list, cell_in, mix_in, held, sems):
    lines, shards, per_shard, pair_dev = sizes
    line, shard = lax.axis_index("grp"), lax.axis_index("shard")
    copy_cell = pltpu.make_async_copy(w_cell, cell_in, sems.at[0])
    copy_pairs = pltpu.make_async_copy(pairs, held, sems.at[1])
    copy_mix = pltpu.make_async_copy(w_mix, mix_in, sems.at[2])
    copy_pairs.start()
    copy_cell.start()
    copy_mix.start()
    copy_pairs.wait()
    slot = lax.broadcasted_iota(jnp.int32, ids.shape, 1)
    a, b = held[:1], held[1:]
    live = slot < counts[0]
    ids[...] = jnp.where(live, a * (shards * per_shard) + b, -1)
    mine = live & (b // (2 * per_shard) == shard // 2)
    x = lax.rem(a, per_shard)
    y = lax.rem(b, per_shard) + per_shard * lax.rem(b // per_shard + shard, 2)
    reader = jnp.full_like(slot, line * shards + shard)
    own_list[...] = pack_list(mine, (x, y, reader, slot), own_list.shape[1])
    copy_cell.wait()
    copy_mix.wait()


def pack_list(mine, values, lanes):
    rows, slots = mine.shape
    earlier = (
        lax.broadcasted_iota(jnp.int32, (slots, slots), 0)
        < lax.broadcasted_iota(jnp.int32, (slots, slots), 1)
    ).astype(BF16)
    place = lax.broadcasted_iota(jnp.int32, (lanes, slots), 0)
    field = lax.broadcasted_iota(jnp.int32, (8, slots), 0)
    before = dot(mine.astype(BF16), earlier)
    row_total = jnp.sum(mine.astype(F32), axis=1, keepdims=True)
    total = jnp.zeros((1, 1), F32)
    packed = jnp.zeros((8, lanes), F32)
    for r in range(rows):
        position = (before[r : r + 1] + total).astype(jnp.int32)
        position = jnp.where(mine[r : r + 1], position, -1)
        total = total + row_total[r : r + 1]
        chosen = (place == position).astype(BF16)
        fields = jnp.zeros_like(field)
        for which, value in enumerate(values):
            fields = jnp.where(field == which, value[r : r + 1], fields)
        packed = packed + dot_nt(fields.astype(BF16), chosen)
    packed = packed.astype(jnp.int32)
    code = packed[:1]
    for which in range(1, len(values)):
        code = code + packed[which : which + 1] * 2 ** (which * CODE_BITS)
    return jnp.concatenate([code, jnp.broadcast_to(total, code.shape).astype(jnp.int32)], axis=0)


def route_kernel(sizes, whose, *refs):
    lines, shards, per_shard, pair_dev = sizes
    ids_refs, out_refs = refs[:lines], refs[lines + 1 :]
    total_columns = shards * per_shard
    chip_columns = 2 * per_shard
    chips = shards // 2
    quarter = per_shard // lines
    line = lax.axis_index("grp")
    shard = lax.axis_index("shard")
    chip, core = shard // 2, lax.rem(shard, 2)
    ids = jnp.concatenate([ref[...] for ref in ids_refs], axis=0)
    live = ids >= 0
    kept = jnp.maximum(ids, 0)
    a = kept // total_columns
    b = kept - a * total_columns
    b_chip = b // chip_columns
    b_shard = b // per_shard
    a_local = lax.rem(a, per_shard)
    b_local = lax.rem(b, per_shard)
    reader_row = lax.broadcasted_iota(jnp.int32, ids.shape, 0)
    reader_id = lax.rem(line + reader_row, lines) * shards + shard
    slot = lax.broadcasted_iota(jnp.int32, ids.shape, 1)
    b_own = b_local + per_shard * lax.rem(b_shard + core, 2)
    lanes = out_refs[0].shape[1]
    for group, out_ref in zip(whose, out_refs):
        for at, (kind, offset) in enumerate(group):
            base = chip_columns + (offset - 1) * quarter
            if kind in ("receive", "partner"):
                here = core if kind == "receive" else 1 - core
                source = ring_place(chip, chips, offset)
                mine = live & (b_shard == source * 2 + here) & (b_local // quarter == line)
                x = a_local if kind == "receive" else a_local + per_shard
                y = base + b_local - line * quarter
            else:
                target = ring_place(chip, chips, -offset)
                mine = live & (b_chip == target) & (a_local // quarter == line)
                x, y = b_own, base + a_local - line * quarter
            out_ref[2 * at : 2 * at + 2] = pack_list(mine, (x, y, reader_id, slot), lanes)


def ring_place(chip, chips, offset):
    half = chips // 2
    place = jnp.where(chip < half, 2 * chip, 2 * (chip - half) + 1)
    other = lax.rem(place + offset + 2 * chips, chips)
    return other // 2 + half * lax.rem(other, 2)


def ring_of(chips):
    half = chips // 2
    return [p // 2 + half * (p % 2) for p in range(chips)]


def local(mesh_shape, cells, w_cell, w_mix, w_pool, pairs, counts):
    lines, shards = mesh_shape["grp"], mesh_shape["shard"]
    chips = shards // 2
    per_shard, samples, width = cells.shape
    pair_dev = pairs.shape[0]
    quarter = per_shard // lines
    score_scale = 1.0 / math.sqrt(width)
    ring = ring_of(chips)

    def from_ahead(offset):
        return [
            (2 * ring[(p + offset) % chips] + c, 2 * ring[p] + c) for p in range(chips) for c in (0, 1)
        ]

    offsets = range(1, chips // 2 + 1)
    swap = [(s, s ^ 1) for s in range(shards)]
    sizes = (lines, shards, per_shard, pair_dev)
    assert max(2 * per_shard + len(offsets) * quarter, lines * shards) <= 2**CODE_BITS
    assert pair_dev <= 2 ** (31 - 3 * CODE_BITS)
    most = lines * min(pair_dev, 4 * pair_dev // shards)
    lanes = -(-max(most, pair_dev) // LANES) * LANES
    weight = jax.ShapeDtypeStruct(w_cell.shape, BF16)
    weight_bytes = 2 * width * width
    share = pl.pallas_call(
        share_kernel,
        out_shape=jax.ShapeDtypeStruct((quarter, samples, width), BF16),
        in_specs=[hbm()],
        out_specs=vmem(),
        scratch_shapes=[pltpu.SemaphoreType.DMA(())],
        compiler_params=pltpu.CompilerParams(vmem_limit_bytes=4 * 2**20),
        name="share",
    )(in_hbm(cells))
    remote = {d: lax.ppermute(share, "shard", from_ahead(d)) for d in offsets}
    cells, _ = lax.optimization_barrier((cells, share))
    partner = lax.ppermute(cells, "shard", swap)
    ids, own_list, w_cell, w_mix = pl.pallas_call(
        functools.partial(prepare_kernel, sizes),
        out_shape=(
            jax.ShapeDtypeStruct((1, pair_dev), jnp.int32),
            jax.ShapeDtypeStruct((2, lanes), jnp.int32),
            weight,
            weight,
        ),
        in_specs=[hbm(), smem(), hbm(), hbm(), pl.BlockSpec(memory_space=pl.ANY)],
        out_specs=[vmem()] * 4,
        scratch_shapes=[pltpu.VMEM((2, pair_dev), jnp.int32), pltpu.SemaphoreType.DMA((3,))],
        compiler_params=pltpu.CompilerParams(vmem_limit_bytes=2 * weight_bytes + 4 * 2**20),
        name="prepare",
    )(in_hbm(pairs.T), counts, in_hbm(w_cell), in_hbm(w_mix), share)
    ids = [ids] + [
        lax.ppermute(ids, "grp", [((g + k) % lines, g) for g in range(lines)])
        for k in range(1, lines)
    ]

    store = jax.ShapeDtypeStruct((2 * per_shard + len(offsets) * quarter, samples, width), BF16)
    scores = jax.ShapeDtypeStruct((lines * shards, pair_dev), F32)
    store_bytes = 2 * math.prod(store.shape)
    weight_bytes = 2 * width * width

    def pools(count):
        rows = count * lanes + LANES
        return [jax.ShapeDtypeStruct((rows, n), F32) for n in (width + LANES, width)]

    def limit(spare):
        return pltpu.CompilerParams(
            vmem_limit_bytes=2 * store_bytes + 3 * weight_bytes + spare * 2**20
        )

    proj, mixed = pl.pallas_call(
        project_kernel,
        out_shape=[store, store],
        in_specs=[hbm()] + [vmem()] * 3,
        out_specs=[vmem()] * 2,
        scratch_shapes=[pltpu.VMEM(cells.shape, BF16), pltpu.SemaphoreType.DMA(())],
        compiler_params=limit(16),
        name="project",
    )(in_hbm(cells), partner, w_cell, w_mix)

    groups = [offsets[i : i + 2] for i in range(0, len(offsets), 2)]
    whose, spans = [], []
    for group in groups:
        near = [[(kind, d) for d in group] for kind in ("receive", "partner")]
        far = [[("send", d)] for d in group if 2 * d != chips]
        spans.append((len(whose), len(whose) + len(near), len(whose) + len(near + far)))
        whose += near + far
    lists = pl.pallas_call(
        functools.partial(route_kernel, sizes, whose),
        out_shape=[jax.ShapeDtypeStruct((2 * len(kinds), lanes), jnp.int32) for kinds in whose],
        in_specs=[vmem()] * lines + [pl.BlockSpec(memory_space=pl.ANY)],
        out_specs=[vmem()] * len(whose),
        compiler_params=pltpu.CompilerParams(vmem_limit_bytes=4 * 2**20),
        name="route",
    )(*ids, proj)
    arrived = []
    for kinds, packed in zip(whose, lists):
        kind, d = kinds[0]
        if kind == "partner":
            packed = lax.ppermute(packed, "shard", swap)
        elif kind == "send":
            packed = lax.ppermute(packed, "shard", from_ahead(d))
        arrived.append(packed)

    out, w_pool = pl.pallas_call(
        functools.partial(chip_kernel, score_scale),
        out_shape=[scores, weight],
        in_specs=[smem(), vmem(), vmem(), hbm(), pl.BlockSpec(memory_space=pl.ANY)],
        out_specs=[vmem()] * 2,
        scratch_shapes=[
            *(pltpu.VMEM(x.shape, F32) for x in pools(1)),
            pltpu.SemaphoreType.DMA(()),
        ],
        compiler_params=limit(16),
        name="chip",
    )(own_list, proj, mixed, in_hbm(w_pool), lists[-1])

    for group, (first, middle, last) in zip(groups, spans):
        use = arrived[first:last]
        held = [x.shape[0] // 2 for x in use]
        number = middle - first
        at = number + len(group) + 2
        proj, mixed, *pooled = pl.pallas_call(
            functools.partial(
                near_kernel,
                len(group),
                2 * per_shard + (group[0] - 1) * quarter,
                held[:number],
                score_scale,
            ),
            out_shape=[store, store, *pools(sum(held))],
            in_specs=[vmem()] * (number + len(group) + 4),
            out_specs=[vmem()] * 4,
            input_output_aliases={at: 0, at + 1: 1},
            scratch_shapes=[
                *(pltpu.SMEM(x.shape, jnp.int32) for x in use[:number]),
                pltpu.SemaphoreType.DMA((number,)),
            ],
            compiler_params=limit(20),
            name="near" + "_".join(map(str, group)),
        )(*use[:number], *(remote[d] for d in group), w_cell, w_mix, proj, mixed)
        at = len(use) + 3
        out, *_ = pl.pallas_call(
            functools.partial(far_kernel, held, sum(held[:number]), score_scale),
            out_shape=[scores, *pools(sum(held))],
            in_specs=[vmem()] * (len(use) + 6),
            out_specs=[vmem()] * 3,
            input_output_aliases={at: 0, at + 1: 1, at + 2: 2},
            scratch_shapes=[
                *(pltpu.SMEM(x.shape, jnp.int32) for x in use),
                pltpu.SemaphoreType.DMA((len(use),)),
            ],
            compiler_params=limit(20),
            name="far" + "_".join(map(str, group)),
        )(*use, proj, mixed, w_pool, out, *pooled)

    back = lax.all_to_all(out, ("grp", "shard"), 0, 0, tiled=True)
    return jnp.sum(back, axis=0)


def solution(mesh):
    placed = (P("shard", None, None), P(), P(), P(), P(("grp", "shard"), None), P(("grp", "shard")))
    return jax.shard_map(
        functools.partial(local, dict(mesh.shape)),
        mesh=mesh,
        in_specs=placed,
        out_specs=P(("grp", "shard")),
        check_vma=False,
    )
```

```python
import functools
import math

import jax
import jax.numpy as jnp
from jax import lax
from jax.experimental import pallas as pl
from jax.experimental.pallas import tpu as pltpu
from jax.sharding import PartitionSpec as P

SOFTMAX_WARMTH = 0.07
EPSILON = 1e-06
LANES = 128
STEPS = (16, 8, 4)
F32 = jnp.float32
BF16 = jnp.bfloat16
NT = (((1,), (1,)), ((), ()))
CODE_BITS = 8


def vmem():
    return pl.BlockSpec(memory_space=pltpu.VMEM)


def hbm():
    return pl.BlockSpec(memory_space=pltpu.HBM)


def in_hbm(x):
    return pltpu.with_memory_space_constraint(x, pltpu.HBM)


def smem():
    return pl.BlockSpec(memory_space=pltpu.SMEM)


def dot(a, b):
    return jnp.dot(a, b, preferred_element_type=F32)


def dot_nt(a, b):
    return lax.dot_general(a, b, NT, preferred_element_type=F32)


def first_projection(block, w_cell, proj, at):
    columns, samples, width = block.shape
    rows = dot(block.reshape(-1, width), w_cell[...]).astype(BF16)
    proj[at : at + columns] = rows.reshape(columns, samples, width)
    return rows


def second_projection(rows, w_mix, mixed, at):
    _, samples, width = mixed.shape
    mixed[at : at + rows.shape[0] // samples] = (
        dot(rows, w_mix[...]).astype(BF16).reshape(-1, samples, width)
    )


def project_kernel(own, partner, w_cell, w_mix, proj, mixed, own_in, sem):
    columns = own.shape[0]
    copy = pltpu.make_async_copy(own, own_in, sem)
    copy.start()
    rows = first_projection(partner[...], w_cell, proj, columns)
    second_projection(rows, w_mix, mixed, columns)
    copy.wait()
    rows = first_projection(own_in[...], w_cell, proj, 0)
    second_projection(rows, w_mix, mixed, 0)


def chip_kernel(score_scale, index, proj, mixed, w_pool, _, out, pool_in, pool_x, pool_y, sem):
    copy = pltpu.make_async_copy(w_pool, pool_in, sem)
    copy.start()
    out[...] = jnp.zeros(out.shape, F32)
    lists = [(index, 0)]
    attend_lists(lists, 0, proj, mixed, score_scale, pool_x, pool_y)
    copy.wait()
    score_lists(lists, pool_in, out, pool_x, pool_y)


def attend_pairs(pairs, proj, mixed, score_scale):
    samples = proj.shape[1]
    shape = (samples, 2 * samples)
    lane = lax.broadcasted_iota(jnp.int32, shape, 1)
    first = lane < samples
    unit = (lax.rem(lane, samples) == lax.broadcasted_iota(jnp.int32, shape, 0)).astype(F32)
    weights, attend, pooled = [], [], []

    def score(x, y):
        both = dot_nt(
            jnp.concatenate([proj[y], proj[x]], axis=0), jnp.concatenate([proj[x], proj[y]], axis=0)
        )
        weights.append(jnp.where(first, both[:samples], both[samples:]) * score_scale)

    def soften(w):
        w = jnp.exp(w - jnp.max(w, axis=0, keepdims=True))
        w = w * (1.0 / jnp.sum(w, axis=0, keepdims=True))
        blocks = [jnp.where(first, w, unit), jnp.where(first, unit, w)]
        attend.append(jnp.transpose(jnp.concatenate(blocks, axis=0)).astype(BF16))

    def mix(t, x, y):
        rows = jnp.tanh(dot(t, jnp.concatenate([mixed[y], mixed[x]], axis=0)))
        pooled.append(
            [jnp.sum(r, axis=0, keepdims=True) * (1.0 / samples) for r in (rows[:samples], rows[samples:])]
        )

    group = STEPS[-1]
    for at in range(len(pairs) + 2 * group):
        early, late = at - group, at - 2 * group
        if late >= 0:
            mix(attend[late], *pairs[late])
        if at < len(pairs):
            score(*pairs[at])
        if 0 <= early < len(pairs):
            soften(weights[early])
    return pooled


def lists_of(held, index):
    return [(ref, 2 * at) for ref, number in zip(index, held) for at in range(number)]


def start_copies(sources, targets, sems):
    copies = [
        pltpu.make_async_copy(source, target, sems.at[i])
        for i, (source, target) in enumerate(zip(sources, targets))
    ]
    for copy in copies:
        copy.start()
    return copies


def near_kernel(chips, base, held, score_scale, *refs):
    count = len(held)
    lists, remote = refs[:count], refs[count : count + chips]
    w_cell, w_mix, _, _, proj, mixed, pool_x, pool_y = refs[count + chips : -1 - count]
    index, sems = refs[-1 - count : -1], refs[-1]
    copies = start_copies(lists, index, sems)
    places = [base + i * remote[0].shape[0] for i in range(chips)]
    rows = [first_projection(ref[...], w_cell, proj, at) for ref, at in zip(remote, places)]
    for block, at in zip(rows, places):
        second_projection(block, w_mix, mixed, at)
    for copy in copies:
        copy.wait()
    attend_lists(lists_of(held, index), 0, proj, mixed, score_scale, pool_x, pool_y, last=False)


def far_kernel(held, near, score_scale, *refs):
    count = len(held)
    lists = refs[:count]
    proj, mixed, w_pool, before, _, _, out, pool_x, pool_y = refs[count : -1 - count]
    index, sems = refs[-1 - count : -1], refs[-1]
    copies = start_copies(lists, index, sems)
    out[...] = before[...]
    for copy in copies:
        copy.wait()
    every = lists_of(held, index)
    attend_lists(every, near, proj, mixed, score_scale, pool_x, pool_y)
    score_lists(every, w_pool, out, pool_x, pool_y)


def starts_of(lists):
    starts = [0]
    for ref, row in lists:
        starts.append(starts[-1] + ref[row + 1, 0])
    return starts


def attend_lists(lists, near, proj, mixed, score_scale, pool_x, pool_y, last=True):
    lanes = lists[0][0].shape[1]
    starts = starts_of(lists)
    todo = list(zip(lists, starts))
    lane = lax.broadcasted_iota(jnp.int32, (1, LANES), 1)

    def column(at):
        code = 0
        for (ref, row), start in todo:
            here = jnp.clip(at - start, 0, lanes - 1)
            code = jnp.where(at >= start, ref[row, here], code)
        mask = 2**CODE_BITS - 1
        return (
            code & mask,
            (code >> CODE_BITS) & mask,
            (code >> 2 * CODE_BITS) & mask,
            code >> 3 * CODE_BITS,
        )

    def step(first, size, i, carry):
        at = [first + i * size + u for u in range(size)]
        columns = [column(p) for p in at]
        pooled = attend_pairs([(x, y) for x, y, _, _ in columns], proj, mixed, score_scale)
        for p, (_, _, reader, slot), (row_x, row_y) in zip(at, columns, pooled):
            tag = jnp.where(lane == 0, reader, slot).astype(F32)
            pool_x[pl.ds(p, 1)] = jnp.concatenate([row_x, tag], axis=1)
            pool_y[pl.ds(p, 1)] = row_y
        return carry

    large, middle, small = STEPS
    first = starts[near] // large * large
    left = starts[-1] - first
    rest = lax.rem(left, large) if last else jnp.int32(0)
    counts = (
        left // large + (rest > middle + small).astype(jnp.int32),
        ((rest > small) & (rest <= middle + small)).astype(jnp.int32),
        (((rest > 0) & (rest <= small)) | ((rest > middle) & (rest <= middle + small))).astype(jnp.int32),
    )
    for size, count in zip(STEPS if last else STEPS[:1], counts):
        lax.fori_loop(0, count, functools.partial(step, first, size), 0)
        first = first + size * count


def score_lists(lists, w_pool, out, pool_x, pool_y):
    total = starts_of(lists)[-1]
    block = LANES // 2
    width = w_pool.shape[0]
    readers, slots = out.shape

    def step(i, carry):
        here = pl.ds(pl.multiple_of(i * block, block), block)
        pooled = jnp.concatenate([pool_x[here, :width], pool_y[here]], axis=0).astype(BF16)
        z = dot(pooled, w_pool[...])
        zx, zy = z[:block], z[block:]
        inner = jnp.mean(zx * zy, axis=1, keepdims=True)
        norms = (jnp.mean(zx * zx, axis=1, keepdims=True) + EPSILON) * (
            jnp.mean(zy * zy, axis=1, keepdims=True) + EPSILON
        )
        score = inner / jnp.sqrt(norms) / SOFTMAX_WARMTH
        live = lax.broadcasted_iota(jnp.int32, (block, 1), 0) < total - i * block
        tags = jnp.where(live, pool_x[here, width:], -1.0).astype(jnp.int32)
        score = jnp.where(live, score, 0.0)
        of_reader = tags[:, :1] == lax.broadcasted_iota(jnp.int32, (block, readers), 1)
        of_slot = tags[:, 1:2] == lax.broadcasted_iota(jnp.int32, (block, slots), 1)
        out[...] += lax.dot_general(
            jnp.where(of_reader, score, 0.0),
            of_slot.astype(F32),
            (((0,), (0,)), ((), ())),
            preferred_element_type=F32,
            precision=lax.Precision.HIGHEST,
        )
        return carry

    lax.fori_loop(0, (total + block - 1) // block, step, 0)


def share_kernel(cells, share, sem):
    quarter = share.shape[0]
    first = lax.axis_index("grp") * quarter
    copy = pltpu.make_async_copy(cells.at[pl.ds(first, quarter)], share, sem)
    copy.start()
    copy.wait()


def prepare_kernel(sizes, pairs, counts, w_cell, w_mix, _, ids, own_list, cell_in, mix_in, held, sems):
    lines, shards, per_shard, pair_dev = sizes
    line, shard = lax.axis_index("grp"), lax.axis_index("shard")
    copy_cell = pltpu.make_async_copy(w_cell, cell_in, sems.at[0])
    copy_pairs = pltpu.make_async_copy(pairs, held, sems.at[1])
    copy_mix = pltpu.make_async_copy(w_mix, mix_in, sems.at[2])
    copy_pairs.start()
    copy_cell.start()
    copy_mix.start()
    copy_pairs.wait()
    slot = lax.broadcasted_iota(jnp.int32, ids.shape, 1)
    a, b = held[:1], held[1:]
    live = slot < counts[0]
    ids[...] = jnp.where(live, a * (shards * per_shard) + b, -1)
    mine = live & (b // (2 * per_shard) == shard // 2)
    x = lax.rem(a, per_shard)
    y = lax.rem(b, per_shard) + per_shard * lax.rem(b // per_shard + shard, 2)
    reader = jnp.full_like(slot, line * shards + shard)
    own_list[...] = pack_list(mine, (x, y, reader, slot), own_list.shape[1])
    copy_cell.wait()
    copy_mix.wait()


def pack_list(mine, values, lanes):
    rows, slots = mine.shape
    earlier = (
        lax.broadcasted_iota(jnp.int32, (slots, slots), 0)
        < lax.broadcasted_iota(jnp.int32, (slots, slots), 1)
    ).astype(BF16)
    place = lax.broadcasted_iota(jnp.int32, (lanes, slots), 0)
    field = lax.broadcasted_iota(jnp.int32, (8, slots), 0)
    before = dot(mine.astype(BF16), earlier)
    row_total = jnp.sum(mine.astype(F32), axis=1, keepdims=True)
    total = jnp.zeros((1, 1), F32)
    packed = jnp.zeros((8, lanes), F32)
    for r in range(rows):
        position = (before[r : r + 1] + total).astype(jnp.int32)
        position = jnp.where(mine[r : r + 1], position, -1)
        total = total + row_total[r : r + 1]
        chosen = (place == position).astype(BF16)
        fields = jnp.zeros_like(field)
        for which, value in enumerate(values):
            fields = jnp.where(field == which, value[r : r + 1], fields)
        packed = packed + dot_nt(fields.astype(BF16), chosen)
    packed = packed.astype(jnp.int32)
    code = packed[:1]
    for which in range(1, len(values)):
        code = code + packed[which : which + 1] * 2 ** (which * CODE_BITS)
    return jnp.concatenate([code, jnp.broadcast_to(total, code.shape).astype(jnp.int32)], axis=0)


def route_kernel(sizes, whose, *refs):
    lines, shards, per_shard, pair_dev = sizes
    ids_refs, out_refs = refs[:lines], refs[lines + 1 :]
    total_columns = shards * per_shard
    chip_columns = 2 * per_shard
    chips = shards // 2
    quarter = per_shard // lines
    line = lax.axis_index("grp")
    shard = lax.axis_index("shard")
    chip, core = shard // 2, lax.rem(shard, 2)
    ids = jnp.concatenate([ref[...] for ref in ids_refs], axis=0)
    live = ids >= 0
    kept = jnp.maximum(ids, 0)
    a = kept // total_columns
    b = kept - a * total_columns
    b_chip = b // chip_columns
    b_shard = b // per_shard
    a_local = lax.rem(a, per_shard)
    b_local = lax.rem(b, per_shard)
    reader_row = lax.broadcasted_iota(jnp.int32, ids.shape, 0)
    reader_id = lax.rem(line + reader_row, lines) * shards + shard
    slot = lax.broadcasted_iota(jnp.int32, ids.shape, 1)
    b_own = b_local + per_shard * lax.rem(b_shard + core, 2)
    lanes = out_refs[0].shape[1]
    for group, out_ref in zip(whose, out_refs):
        for at, (kind, offset) in enumerate(group):
            base = chip_columns + (offset - 1) * quarter
            if kind in ("receive", "partner"):
                here = core if kind == "receive" else 1 - core
                source = ring_place(chip, chips, offset)
                mine = live & (b_shard == source * 2 + here) & (b_local // quarter == line)
                x = a_local if kind == "receive" else a_local + per_shard
                y = base + b_local - line * quarter
            else:
                target = ring_place(chip, chips, -offset)
                mine = live & (b_chip == target) & (a_local // quarter == line)
                x, y = b_own, base + a_local - line * quarter
            out_ref[2 * at : 2 * at + 2] = pack_list(mine, (x, y, reader_id, slot), lanes)


def ring_place(chip, chips, offset):
    half = chips // 2
    place = jnp.where(chip < half, 2 * chip, 2 * (chip - half) + 1)
    other = lax.rem(place + offset + 2 * chips, chips)
    return other // 2 + half * lax.rem(other, 2)


def ring_of(chips):
    half = chips // 2
    return [p // 2 + half * (p % 2) for p in range(chips)]


def local(mesh_shape, cells, w_cell, w_mix, w_pool, pairs, counts):
    lines, shards = mesh_shape["grp"], mesh_shape["shard"]
    chips = shards // 2
    per_shard, samples, width = cells.shape
    pair_dev = pairs.shape[0]
    quarter = per_shard // lines
    score_scale = 1.0 / math.sqrt(width)
    ring = ring_of(chips)

    def from_ahead(offset):
        return [
            (2 * ring[(p + offset) % chips] + c, 2 * ring[p] + c) for p in range(chips) for c in (0, 1)
        ]

    offsets = range(1, chips // 2 + 1)
    swap = [(s, s ^ 1) for s in range(shards)]
    sizes = (lines, shards, per_shard, pair_dev)
    assert max(2 * per_shard + len(offsets) * quarter, lines * shards) <= 2**CODE_BITS
    assert pair_dev <= 2 ** (31 - 3 * CODE_BITS)
    most = lines * min(pair_dev, 4 * pair_dev // shards)
    lanes = -(-max(most, pair_dev) // LANES) * LANES
    weight = jax.ShapeDtypeStruct(w_cell.shape, BF16)
    weight_bytes = 2 * width * width
    share = pl.pallas_call(
        share_kernel,
        out_shape=jax.ShapeDtypeStruct((quarter, samples, width), BF16),
        in_specs=[hbm()],
        out_specs=vmem(),
        scratch_shapes=[pltpu.SemaphoreType.DMA(())],
        compiler_params=pltpu.CompilerParams(vmem_limit_bytes=4 * 2**20),
        name="share",
    )(in_hbm(cells))
    remote = {d: lax.ppermute(share, "shard", from_ahead(d)) for d in offsets}
    cells, _ = lax.optimization_barrier((cells, share))
    partner = lax.ppermute(cells, "shard", swap)
    ids, own_list, w_cell, w_mix = pl.pallas_call(
        functools.partial(prepare_kernel, sizes),
        out_shape=(
            jax.ShapeDtypeStruct((1, pair_dev), jnp.int32),
            jax.ShapeDtypeStruct((2, lanes), jnp.int32),
            weight,
            weight,
        ),
        in_specs=[hbm(), smem(), hbm(), hbm(), pl.BlockSpec(memory_space=pl.ANY)],
        out_specs=[vmem()] * 4,
        scratch_shapes=[pltpu.VMEM((2, pair_dev), jnp.int32), pltpu.SemaphoreType.DMA((3,))],
        compiler_params=pltpu.CompilerParams(vmem_limit_bytes=2 * weight_bytes + 4 * 2**20),
        name="prepare",
    )(in_hbm(pairs.T), counts, in_hbm(w_cell), in_hbm(w_mix), share)
    ids = [ids] + [
        lax.ppermute(ids, "grp", [((g + k) % lines, g) for g in range(lines)])
        for k in range(1, lines)
    ]

    store = jax.ShapeDtypeStruct((2 * per_shard + len(offsets) * quarter, samples, width), BF16)
    scores = jax.ShapeDtypeStruct((lines * shards, pair_dev), F32)
    store_bytes = 2 * math.prod(store.shape)
    weight_bytes = 2 * width * width

    def pools(count):
        rows = count * lanes + LANES
        return [jax.ShapeDtypeStruct((rows, n), F32) for n in (width + LANES, width)]

    def limit(spare):
        return pltpu.CompilerParams(
            vmem_limit_bytes=2 * store_bytes + 3 * weight_bytes + spare * 2**20
        )

    proj, mixed = pl.pallas_call(
        project_kernel,
        out_shape=[store, store],
        in_specs=[hbm()] + [vmem()] * 3,
        out_specs=[vmem()] * 2,
        scratch_shapes=[pltpu.VMEM(cells.shape, BF16), pltpu.SemaphoreType.DMA(())],
        compiler_params=limit(16),
        name="project",
    )(in_hbm(cells), partner, w_cell, w_mix)

    groups = [offsets[i : i + 2] for i in range(0, len(offsets), 2)]
    whose, spans = [], []
    for group in groups:
        near = [[(kind, d) for d in group] for kind in ("receive", "partner")]
        far = [[("send", d)] for d in group if 2 * d != chips]
        spans.append((len(whose), len(whose) + len(near), len(whose) + len(near + far)))
        whose += near + far
    lists = pl.pallas_call(
        functools.partial(route_kernel, sizes, whose),
        out_shape=[jax.ShapeDtypeStruct((2 * len(kinds), lanes), jnp.int32) for kinds in whose],
        in_specs=[vmem()] * lines + [pl.BlockSpec(memory_space=pl.ANY)],
        out_specs=[vmem()] * len(whose),
        compiler_params=pltpu.CompilerParams(vmem_limit_bytes=4 * 2**20),
        name="route",
    )(*ids, proj)
    arrived = []
    for kinds, packed in zip(whose, lists):
        kind, d = kinds[0]
        if kind == "partner":
            packed = lax.ppermute(packed, "shard", swap)
        elif kind == "send":
            packed = lax.ppermute(packed, "shard", from_ahead(d))
        arrived.append(packed)

    out, w_pool = pl.pallas_call(
        functools.partial(chip_kernel, score_scale),
        out_shape=[scores, weight],
        in_specs=[smem(), vmem(), vmem(), hbm(), pl.BlockSpec(memory_space=pl.ANY)],
        out_specs=[vmem()] * 2,
        scratch_shapes=[
            *(pltpu.VMEM(x.shape, F32) for x in pools(1)),
            pltpu.SemaphoreType.DMA(()),
        ],
        compiler_params=limit(16),
        name="chip",
    )(own_list, proj, mixed, in_hbm(w_pool), lists[-1])

    for group, (first, middle, last) in zip(groups, spans):
        use = arrived[first:last]
        held = [x.shape[0] // 2 for x in use]
        number = middle - first
        at = number + len(group) + 2
        proj, mixed, *pooled = pl.pallas_call(
            functools.partial(
                near_kernel,
                len(group),
                2 * per_shard + (group[0] - 1) * quarter,
                held[:number],
                score_scale,
            ),
            out_shape=[store, store, *pools(sum(held))],
            in_specs=[vmem()] * (number + len(group) + 4),
            out_specs=[vmem()] * 4,
            input_output_aliases={at: 0, at + 1: 1},
            scratch_shapes=[
                *(pltpu.SMEM(x.shape, jnp.int32) for x in use[:number]),
                pltpu.SemaphoreType.DMA((number,)),
            ],
            compiler_params=limit(20),
            name="near" + "_".join(map(str, group)),
        )(*use[:number], *(remote[d] for d in group), w_cell, w_mix, proj, mixed)
        at = len(use) + 3
        out, *_ = pl.pallas_call(
            functools.partial(far_kernel, held, sum(held[:number]), score_scale),
            out_shape=[scores, *pools(sum(held))],
            in_specs=[vmem()] * (len(use) + 6),
            out_specs=[vmem()] * 3,
            input_output_aliases={at: 0, at + 1: 1, at + 2: 2},
            scratch_shapes=[
                *(pltpu.SMEM(x.shape, jnp.int32) for x in use),
                pltpu.SemaphoreType.DMA((len(use),)),
            ],
            compiler_params=limit(20),
            name="far" + "_".join(map(str, group)),
        )(*use, proj, mixed, w_pool, out, *pooled)

    back = lax.all_to_all(out, ("grp", "shard"), 0, 0, tiled=True)
    return jnp.sum(back, axis=0)


def solution(mesh):
    placed = (P("shard", None, None), P(), P(), P(), P(("grp", "shard"), None), P(("grp", "shard")))
    return jax.shard_map(
        functools.partial(local, dict(mesh.shape)),
        mesh=mesh,
        in_specs=placed,
        out_specs=P(("grp", "shard")),
        check_vma=False,
    )
```

```python
import functools
import math

import jax
import jax.numpy as jnp
from jax import lax
from jax.experimental import pallas as pl
from jax.experimental.pallas import tpu as pltpu
from jax.sharding import PartitionSpec as P

SOFTMAX_WARMTH = 0.07
EPSILON = 1e-06
LANES = 128
STEPS = (16, 8, 4)
F32 = jnp.float32
BF16 = jnp.bfloat16
NT = (((1,), (1,)), ((), ()))
CODE_BITS = 8


def vmem():
    return pl.BlockSpec(memory_space=pltpu.VMEM)


def hbm():
    return pl.BlockSpec(memory_space=pltpu.HBM)


def in_hbm(x):
    return pltpu.with_memory_space_constraint(x, pltpu.HBM)


def smem():
    return pl.BlockSpec(memory_space=pltpu.SMEM)


def dot(a, b):
    return jnp.dot(a, b, preferred_element_type=F32)


def dot_nt(a, b):
    return lax.dot_general(a, b, NT, preferred_element_type=F32)


def first_projection(block, w_cell, proj, at):
    columns, samples, width = block.shape
    rows = dot(block.reshape(-1, width), w_cell[...]).astype(BF16)
    proj[at : at + columns] = rows.reshape(columns, samples, width)
    return rows


def second_projection(rows, w_mix, mixed, at):
    _, samples, width = mixed.shape
    mixed[at : at + rows.shape[0] // samples] = (
        dot(rows, w_mix[...]).astype(BF16).reshape(-1, samples, width)
    )


def project_kernel(own, partner, w_cell, w_mix, proj, mixed, own_in, sem):
    columns = own.shape[0]
    copy = pltpu.make_async_copy(own, own_in, sem)
    copy.start()
    rows = first_projection(partner[...], w_cell, proj, columns)
    second_projection(rows, w_mix, mixed, columns)
    copy.wait()
    rows = first_projection(own_in[...], w_cell, proj, 0)
    second_projection(rows, w_mix, mixed, 0)


def chip_kernel(score_scale, index, proj, mixed, w_pool, _, out, pool_in, pool_x, pool_y, sem):
    copy = pltpu.make_async_copy(w_pool, pool_in, sem)
    copy.start()
    out[...] = jnp.zeros(out.shape, F32)
    lists = [(index, 0)]
    attend_lists(lists, 0, proj, mixed, score_scale, pool_x, pool_y)
    copy.wait()
    score_lists(lists, pool_in, out, pool_x, pool_y)


def attend_pairs(pairs, proj, mixed, score_scale):
    samples = proj.shape[1]
    shape = (samples, 2 * samples)
    lane = lax.broadcasted_iota(jnp.int32, shape, 1)
    first = lane < samples
    unit = (lax.rem(lane, samples) == lax.broadcasted_iota(jnp.int32, shape, 0)).astype(F32)
    weights, attend, pooled = [], [], []

    def score(x, y):
        both = dot_nt(
            jnp.concatenate([proj[y], proj[x]], axis=0), jnp.concatenate([proj[x], proj[y]], axis=0)
        )
        weights.append(jnp.where(first, both[:samples], both[samples:]) * score_scale)

    def soften(w):
        w = jnp.exp(w - jnp.max(w, axis=0, keepdims=True))
        w = w * (1.0 / jnp.sum(w, axis=0, keepdims=True))
        blocks = [jnp.where(first, w, unit), jnp.where(first, unit, w)]
        attend.append(jnp.transpose(jnp.concatenate(blocks, axis=0)).astype(BF16))

    def mix(t, x, y):
        rows = jnp.tanh(dot(t, jnp.concatenate([mixed[y], mixed[x]], axis=0)))
        pooled.append(
            [jnp.sum(r, axis=0, keepdims=True) * (1.0 / samples) for r in (rows[:samples], rows[samples:])]
        )

    group = STEPS[-1]
    for at in range(len(pairs) + 2 * group):
        early, late = at - group, at - 2 * group
        if late >= 0:
            mix(attend[late], *pairs[late])
        if at < len(pairs):
            score(*pairs[at])
        if 0 <= early < len(pairs):
            soften(weights[early])
    return pooled


def lists_of(held, index):
    return [(ref, 2 * at) for ref, number in zip(index, held) for at in range(number)]


def start_copies(sources, targets, sems):
    copies = [
        pltpu.make_async_copy(source, target, sems.at[i])
        for i, (source, target) in enumerate(zip(sources, targets))
    ]
    for copy in copies:
        copy.start()
    return copies


def near_kernel(chips, base, held, score_scale, *refs):
    count = len(held)
    lists, remote = refs[:count], refs[count : count + chips]
    w_cell, w_mix, _, _, proj, mixed, pool_x, pool_y = refs[count + chips : -1 - count]
    index, sems = refs[-1 - count : -1], refs[-1]
    copies = start_copies(lists, index, sems)
    places = [base + i * remote[0].shape[0] for i in range(chips)]
    rows = [first_projection(ref[...], w_cell, proj, at) for ref, at in zip(remote, places)]
    for block, at in zip(rows, places):
        second_projection(block, w_mix, mixed, at)
    for copy in copies:
        copy.wait()
    attend_lists(lists_of(held, index), 0, proj, mixed, score_scale, pool_x, pool_y, last=False)


def far_kernel(held, near, score_scale, *refs):
    count = len(held)
    lists = refs[:count]
    proj, mixed, w_pool, before, _, _, out, pool_x, pool_y = refs[count : -1 - count]
    index, sems = refs[-1 - count : -1], refs[-1]
    copies = start_copies(lists, index, sems)
    out[...] = before[...]
    for copy in copies:
        copy.wait()
    every = lists_of(held, index)
    attend_lists(every, near, proj, mixed, score_scale, pool_x, pool_y)
    score_lists(every, w_pool, out, pool_x, pool_y)


def starts_of(lists):
    starts = [0]
    for ref, row in lists:
        starts.append(starts[-1] + ref[row + 1, 0])
    return starts


def attend_lists(lists, near, proj, mixed, score_scale, pool_x, pool_y, last=True):
    lanes = lists[0][0].shape[1]
    starts = starts_of(lists)
    todo = list(zip(lists, starts))
    lane = lax.broadcasted_iota(jnp.int32, (1, LANES), 1)

    def column(at):
        code = 0
        for (ref, row), start in todo:
            here = jnp.clip(at - start, 0, lanes - 1)
            code = jnp.where(at >= start, ref[row, here], code)
        mask = 2**CODE_BITS - 1
        return (
            code & mask,
            (code >> CODE_BITS) & mask,
            (code >> 2 * CODE_BITS) & mask,
            code >> 3 * CODE_BITS,
        )

    def step(first, size, i, carry):
        at = [first + i * size + u for u in range(size)]
        columns = [column(p) for p in at]
        pooled = attend_pairs([(x, y) for x, y, _, _ in columns], proj, mixed, score_scale)
        for p, (_, _, reader, slot), (row_x, row_y) in zip(at, columns, pooled):
            tag = jnp.where(lane == 0, reader, slot).astype(F32)
            pool_x[pl.ds(p, 1)] = jnp.concatenate([row_x, tag], axis=1)
            pool_y[pl.ds(p, 1)] = row_y
        return carry

    large, middle, small = STEPS
    first = starts[near] // large * large
    left = starts[-1] - first
    rest = lax.rem(left, large) if last else jnp.int32(0)
    counts = (
        left // large + (rest > middle + small).astype(jnp.int32),
        ((rest > small) & (rest <= middle + small)).astype(jnp.int32),
        (((rest > 0) & (rest <= small)) | ((rest > middle) & (rest <= middle + small))).astype(jnp.int32),
    )
    for size, count in zip(STEPS if last else STEPS[:1], counts):
        lax.fori_loop(0, count, functools.partial(step, first, size), 0)
        first = first + size * count


def score_lists(lists, w_pool, out, pool_x, pool_y):
    total = starts_of(lists)[-1]
    block = LANES // 2
    width = w_pool.shape[0]
    readers, slots = out.shape

    def step(i, carry):
        here = pl.ds(pl.multiple_of(i * block, block), block)
        pooled = jnp.concatenate([pool_x[here, :width], pool_y[here]], axis=0).astype(BF16)
        z = dot(pooled, w_pool[...])
        zx, zy = z[:block], z[block:]
        inner = jnp.mean(zx * zy, axis=1, keepdims=True)
        norms = (jnp.mean(zx * zx, axis=1, keepdims=True) + EPSILON) * (
            jnp.mean(zy * zy, axis=1, keepdims=True) + EPSILON
        )
        score = inner / jnp.sqrt(norms) / SOFTMAX_WARMTH
        live = lax.broadcasted_iota(jnp.int32, (block, 1), 0) < total - i * block
        tags = jnp.where(live, pool_x[here, width:], -1.0).astype(jnp.int32)
        score = jnp.where(live, score, 0.0)
        of_reader = tags[:, :1] == lax.broadcasted_iota(jnp.int32, (block, readers), 1)
        of_slot = tags[:, 1:2] == lax.broadcasted_iota(jnp.int32, (block, slots), 1)
        out[...] += lax.dot_general(
            jnp.where(of_reader, score, 0.0),
            of_slot.astype(F32),
            (((0,), (0,)), ((), ())),
            preferred_element_type=F32,
            precision=lax.Precision.HIGHEST,
        )
        return carry

    lax.fori_loop(0, (total + block - 1) // block, step, 0)


def share_kernel(cells, share, sem):
    quarter = share.shape[0]
    first = lax.axis_index("grp") * quarter
    copy = pltpu.make_async_copy(cells.at[pl.ds(first, quarter)], share, sem)
    copy.start()
    copy.wait()


def prepare_kernel(sizes, pairs, counts, w_cell, w_mix, _, ids, own_list, cell_in, mix_in, held, sems):
    lines, shards, per_shard, pair_dev = sizes
    line, shard = lax.axis_index("grp"), lax.axis_index("shard")
    copy_cell = pltpu.make_async_copy(w_cell, cell_in, sems.at[0])
    copy_pairs = pltpu.make_async_copy(pairs, held, sems.at[1])
    copy_mix = pltpu.make_async_copy(w_mix, mix_in, sems.at[2])
    copy_pairs.start()
    copy_cell.start()
    copy_mix.start()
    copy_pairs.wait()
    slot = lax.broadcasted_iota(jnp.int32, ids.shape, 1)
    a, b = held[:1], held[1:]
    live = slot < counts[0]
    ids[...] = jnp.where(live, a * (shards * per_shard) + b, -1)
    mine = live & (b // (2 * per_shard) == shard // 2)
    x = lax.rem(a, per_shard)
    y = lax.rem(b, per_shard) + per_shard * lax.rem(b // per_shard + shard, 2)
    reader = jnp.full_like(slot, line * shards + shard)
    own_list[...] = pack_list(mine, (x, y, reader, slot), own_list.shape[1])
    copy_cell.wait()
    copy_mix.wait()


def pack_list(mine, values, lanes):
    rows, slots = mine.shape
    earlier = (
        lax.broadcasted_iota(jnp.int32, (slots, slots), 0)
        < lax.broadcasted_iota(jnp.int32, (slots, slots), 1)
    ).astype(BF16)
    place = lax.broadcasted_iota(jnp.int32, (lanes, slots), 0)
    field = lax.broadcasted_iota(jnp.int32, (8, slots), 0)
    before = dot(mine.astype(BF16), earlier)
    row_total = jnp.sum(mine.astype(F32), axis=1, keepdims=True)
    total = jnp.zeros((1, 1), F32)
    packed = jnp.zeros((8, lanes), F32)
    for r in range(rows):
        position = (before[r : r + 1] + total).astype(jnp.int32)
        position = jnp.where(mine[r : r + 1], position, -1)
        total = total + row_total[r : r + 1]
        chosen = (place == position).astype(BF16)
        fields = jnp.zeros_like(field)
        for which, value in enumerate(values):
            fields = jnp.where(field == which, value[r : r + 1], fields)
        packed = packed + dot_nt(fields.astype(BF16), chosen)
    packed = packed.astype(jnp.int32)
    code = packed[:1]
    for which in range(1, len(values)):
        code = code + packed[which : which + 1] * 2 ** (which * CODE_BITS)
    return jnp.concatenate([code, jnp.broadcast_to(total, code.shape).astype(jnp.int32)], axis=0)


def route_kernel(sizes, whose, *refs):
    lines, shards, per_shard, pair_dev = sizes
    ids_refs, out_refs = refs[:lines], refs[lines + 1 :]
    total_columns = shards * per_shard
    chip_columns = 2 * per_shard
    chips = shards // 2
    quarter = per_shard // lines
    line = lax.axis_index("grp")
    shard = lax.axis_index("shard")
    chip, core = shard // 2, lax.rem(shard, 2)
    ids = jnp.concatenate([ref[...] for ref in ids_refs], axis=0)
    live = ids >= 0
    kept = jnp.maximum(ids, 0)
    a = kept // total_columns
    b = kept - a * total_columns
    b_chip = b // chip_columns
    b_shard = b // per_shard
    a_local = lax.rem(a, per_shard)
    b_local = lax.rem(b, per_shard)
    reader_row = lax.broadcasted_iota(jnp.int32, ids.shape, 0)
    reader_id = lax.rem(line + reader_row, lines) * shards + shard
    slot = lax.broadcasted_iota(jnp.int32, ids.shape, 1)
    b_own = b_local + per_shard * lax.rem(b_shard + core, 2)
    lanes = out_refs[0].shape[1]
    for group, out_ref in zip(whose, out_refs):
        for at, (kind, offset) in enumerate(group):
            base = chip_columns + (offset - 1) * quarter
            if kind in ("receive", "partner"):
                here = core if kind == "receive" else 1 - core
                source = ring_place(chip, chips, offset)
                mine = live & (b_shard == source * 2 + here) & (b_local // quarter == line)
                x = a_local if kind == "receive" else a_local + per_shard
                y = base + b_local - line * quarter
            else:
                target = ring_place(chip, chips, -offset)
                mine = live & (b_chip == target) & (a_local // quarter == line)
                x, y = b_own, base + a_local - line * quarter
            out_ref[2 * at : 2 * at + 2] = pack_list(mine, (x, y, reader_id, slot), lanes)


def ring_place(chip, chips, offset):
    half = chips // 2
    place = jnp.where(chip < half, 2 * chip, 2 * (chip - half) + 1)
    other = lax.rem(place + offset + 2 * chips, chips)
    return other // 2 + half * lax.rem(other, 2)


def ring_of(chips):
    half = chips // 2
    return [p // 2 + half * (p % 2) for p in range(chips)]


def local(mesh_shape, cells, w_cell, w_mix, w_pool, pairs, counts):
    lines, shards = mesh_shape["grp"], mesh_shape["shard"]
    chips = shards // 2
    per_shard, samples, width = cells.shape
    pair_dev = pairs.shape[0]
    quarter = per_shard // lines
    score_scale = 1.0 / math.sqrt(width)
    ring = ring_of(chips)

    def from_ahead(offset):
        return [
            (2 * ring[(p + offset) % chips] + c, 2 * ring[p] + c) for p in range(chips) for c in (0, 1)
        ]

    offsets = range(1, chips // 2 + 1)
    swap = [(s, s ^ 1) for s in range(shards)]
    sizes = (lines, shards, per_shard, pair_dev)
    assert max(2 * per_shard + len(offsets) * quarter, lines * shards) <= 2**CODE_BITS
    assert pair_dev <= 2 ** (31 - 3 * CODE_BITS)
    most = lines * min(pair_dev, 4 * pair_dev // shards)
    lanes = -(-max(most, pair_dev) // LANES) * LANES
    weight = jax.ShapeDtypeStruct(w_cell.shape, BF16)
    weight_bytes = 2 * width * width
    share = pl.pallas_call(
        share_kernel,
        out_shape=jax.ShapeDtypeStruct((quarter, samples, width), BF16),
        in_specs=[hbm()],
        out_specs=vmem(),
        scratch_shapes=[pltpu.SemaphoreType.DMA(())],
        compiler_params=pltpu.CompilerParams(vmem_limit_bytes=4 * 2**20),
        name="share",
    )(in_hbm(cells))
    remote = {d: lax.ppermute(share, "shard", from_ahead(d)) for d in offsets}
    partner = lax.ppermute(cells, "shard", swap)
    ids, own_list, w_cell, w_mix = pl.pallas_call(
        functools.partial(prepare_kernel, sizes),
        out_shape=(
            jax.ShapeDtypeStruct((1, pair_dev), jnp.int32),
            jax.ShapeDtypeStruct((2, lanes), jnp.int32),
            weight,
            weight,
        ),
        in_specs=[hbm(), smem(), hbm(), hbm(), pl.BlockSpec(memory_space=pl.ANY)],
        out_specs=[vmem()] * 4,
        scratch_shapes=[pltpu.VMEM((2, pair_dev), jnp.int32), pltpu.SemaphoreType.DMA((3,))],
        compiler_params=pltpu.CompilerParams(vmem_limit_bytes=2 * weight_bytes + 4 * 2**20),
        name="prepare",
    )(in_hbm(pairs.T), counts, in_hbm(w_cell), in_hbm(w_mix), share)
    ids = [ids] + [
        lax.ppermute(ids, "grp", [((g + k) % lines, g) for g in range(lines)])
        for k in range(1, lines)
    ]

    store = jax.ShapeDtypeStruct((2 * per_shard + len(offsets) * quarter, samples, width), BF16)
    scores = jax.ShapeDtypeStruct((lines * shards, pair_dev), F32)
    store_bytes = 2 * math.prod(store.shape)
    weight_bytes = 2 * width * width

    def pools(count):
        rows = count * lanes + LANES
        return [jax.ShapeDtypeStruct((rows, n), F32) for n in (width + LANES, width)]

    def limit(spare):
        return pltpu.CompilerParams(
            vmem_limit_bytes=2 * store_bytes + 3 * weight_bytes + spare * 2**20
        )

    proj, mixed = pl.pallas_call(
        project_kernel,
        out_shape=[store, store],
        in_specs=[hbm()] + [vmem()] * 3,
        out_specs=[vmem()] * 2,
        scratch_shapes=[pltpu.VMEM(cells.shape, BF16), pltpu.SemaphoreType.DMA(())],
        compiler_params=limit(16),
        name="project",
    )(in_hbm(cells), partner, w_cell, w_mix)

    groups = [offsets[i : i + 2] for i in range(0, len(offsets), 2)]
    whose, spans = [], []
    for group in groups:
        near = [[(kind, d) for d in group] for kind in ("receive", "partner")]
        far = [[("send", d)] for d in group if 2 * d != chips]
        spans.append((len(whose), len(whose) + len(near), len(whose) + len(near + far)))
        whose += near + far
    lists = pl.pallas_call(
        functools.partial(route_kernel, sizes, whose),
        out_shape=[jax.ShapeDtypeStruct((2 * len(kinds), lanes), jnp.int32) for kinds in whose],
        in_specs=[vmem()] * lines + [pl.BlockSpec(memory_space=pl.ANY)],
        out_specs=[vmem()] * len(whose),
        compiler_params=pltpu.CompilerParams(vmem_limit_bytes=4 * 2**20),
        name="route",
    )(*ids, proj)
    arrived = []
    for kinds, packed in zip(whose, lists):
        kind, d = kinds[0]
        if kind == "partner":
            packed = lax.ppermute(packed, "shard", swap)
        elif kind == "send":
            packed = lax.ppermute(packed, "shard", from_ahead(d))
        arrived.append(packed)

    out, w_pool = pl.pallas_call(
        functools.partial(chip_kernel, score_scale),
        out_shape=[scores, weight],
        in_specs=[smem(), vmem(), vmem(), hbm(), pl.BlockSpec(memory_space=pl.ANY)],
        out_specs=[vmem()] * 2,
        scratch_shapes=[
            *(pltpu.VMEM(x.shape, F32) for x in pools(1)),
            pltpu.SemaphoreType.DMA(()),
        ],
        compiler_params=limit(16),
        name="chip",
    )(own_list, proj, mixed, in_hbm(w_pool), lists[-1])

    for group, (first, middle, last) in zip(groups, spans):
        use = arrived[first:last]
        held = [x.shape[0] // 2 for x in use]
        number = middle - first
        at = number + len(group) + 2
        proj, mixed, *pooled = pl.pallas_call(
            functools.partial(
                near_kernel,
                len(group),
                2 * per_shard + (group[0] - 1) * quarter,
                held[:number],
                score_scale,
            ),
            out_shape=[store, store, *pools(sum(held))],
            in_specs=[vmem()] * (number + len(group) + 4),
            out_specs=[vmem()] * 4,
            input_output_aliases={at: 0, at + 1: 1},
            scratch_shapes=[
                *(pltpu.SMEM(x.shape, jnp.int32) for x in use[:number]),
                pltpu.SemaphoreType.DMA((number,)),
            ],
            compiler_params=limit(20),
            name="near" + "_".join(map(str, group)),
        )(*use[:number], *(remote[d] for d in group), w_cell, w_mix, proj, mixed)
        at = len(use) + 3
        out, *_ = pl.pallas_call(
            functools.partial(far_kernel, held, sum(held[:number]), score_scale),
            out_shape=[scores, *pools(sum(held))],
            in_specs=[vmem()] * (len(use) + 6),
            out_specs=[vmem()] * 3,
            input_output_aliases={at: 0, at + 1: 1, at + 2: 2},
            scratch_shapes=[
                *(pltpu.SMEM(x.shape, jnp.int32) for x in use),
                pltpu.SemaphoreType.DMA((len(use),)),
            ],
            compiler_params=limit(20),
            name="far" + "_".join(map(str, group)),
        )(*use, proj, mixed, w_pool, out, *pooled)

    back = lax.all_to_all(out, ("grp", "shard"), 0, 0, tiled=True)
    return jnp.sum(back, axis=0)


def solution(mesh):
    placed = (P("shard", None, None), P(), P(), P(), P(("grp", "shard"), None), P(("grp", "shard")))
    return jax.shard_map(
        functools.partial(local, dict(mesh.shape)),
        mesh=mesh,
        in_specs=placed,
        out_specs=P(("grp", "shard")),
        check_vma=False,
    )
```
